256 devices in a mesh: row: 8 (over x, core), col: 32 (over y, z).
Axes of the slice: x: 4, y: 4, z: 8, core: 2. Of those that a mesh axis runs over, the one named last changes fastest.
Arguments:
- rhs: float32 [2048, 16, 8, 512], P('col', None, 'row'), may hold values from -6 to 6
- factor_rows: bfloat16 [2, 512, 16, 8, 512], P(None, 'col', None, 'row'), may hold values from -0.25 to 0.25
- diag_inverse: float32 [2, 512, 512], replicated, may hold values from -1.5 to 1.5, as said below
Outputs:
- solved: float32 [2, 2048, 512], P(None, 'col')
- updated: float32 [2048, 16, 8, 512], P('col', None, 'row')
The draws below stay inside these ranges and needn't reach their ends.
Inputs may be any that keep to these rules, and one draw needn't show every extreme that they name: Each diag_inverse[s] is lower triangular with its diagonal between 0.5 and 1.5.
All inputs are finite; a program needn't handle non-finite values.
Results may differ from the reference program's by a relative error of at most 0.0031.
Values may be sent and summed in bfloat16 or wider, within the bound.
A program may use at most 128 MiB of HBM per device.

```python
import jax
import jax.numpy as jnp
from jax import lax

NB = 512
R = 2048
NBLK_DEV = 16
NBLK = 128
N_ROW = 8


def draw_diag_inverse(key, part):
    key = jax.random.fold_in(key, 7)
    first_key, second_key = jax.random.split(key)
    offdiag = jax.random.normal(first_key, (2, NB, NB), jnp.float32) * 0.5
    offdiag = offdiag * NB ** (-0.5)
    diagonal = jax.random.uniform(second_key, (2, NB), jnp.float32, 0.5, 1.5)
    return jnp.tril(offdiag, -1) + diagonal[:, :, None] * jnp.eye(NB, dtype=jnp.float32)


def shard_levels(own_key, dims, pieces, low, high):
    loudness = 1.0
    for dim, blocks in pieces:
        heights = jax.random.uniform(jax.random.fold_in(jax.random.fold_in(own_key, 6), dim), (blocks,), jnp.float32, low / len(pieces), high / len(pieces))
        loudness = loudness * jnp.repeat(jnp.exp(heights), dims[dim] // blocks).reshape((-1,) + (1,) * (len(dims) - 1 - dim))
    return loudness


def normal_values(rng, extent, deviation, most, cuts=(), kind=jnp.bfloat16):
    loudness = shard_levels(rng, extent, cuts, -0.22, 0.18) if cuts else 1.0
    entries = jax.random.normal(rng, extent, jnp.float32) * deviation * loudness
    return jnp.minimum(jnp.maximum(entries, -most), most).astype(kind)


def setup_inputs(seed: int = 0) -> dict:
    splits = jax.random.split(jax.random.key(seed), 4)
    rhs = normal_values(splits[0], (R, NBLK_DEV, N_ROW, NB), 1.0, 6.0, ((0, 32), (2, 8)), jnp.float32)
    factor_rows = normal_values(splits[1], (2, NB, NBLK_DEV, N_ROW, NB), NB ** -0.5, 0.25, ((1, 32), (3, 8)))
    diag_inverse = draw_diag_inverse(jax.random.fold_in(splits[3], 71), 0)
    return {"rhs": rhs, "factor_rows": factor_rows, "diag_inverse": diag_inverse}


def reference(rhs, factor_rows, diag_inverse):
    pending = rhs.reshape(R, NBLK * NB)
    factor_flat = factor_rows.reshape(2, NB, NBLK * NB)
    column_blocks = jnp.arange(NBLK * NB) // NB
    results = []
    for step_index in range(2):
        current = NBLK - 1 - step_index
        block_rhs = pending[:, current * NB:(current + 1) * NB]
        solution = jnp.dot(block_rhs, diag_inverse[step_index], precision=lax.Precision.HIGHEST, preferred_element_type=jnp.float32)
        narrow = solution.astype(jnp.bfloat16)
        change = jnp.dot(narrow, factor_flat[step_index], preferred_element_type=jnp.float32)
        pending = pending - jnp.where(column_blocks[None, :] < current, change, 0.0)
        results.append(solution)
    return jnp.stack(results), pending.reshape(rhs.shape)
```

```python
import functools

import jax
import jax.numpy as jnp
from jax import lax
from jax.experimental import pallas as pl
from jax.experimental.pallas import tpu as pltpu
from jax.sharding import PartitionSpec as P

NY, NZ, NROW = 4, 8, 8
CHUNKS = 4
BF16, F32 = jnp.bfloat16, jnp.float32


def ring_order():
    hop_us, latency = 1.35, 1.5
    units = [(c, s) for c in range(CHUNKS) for s in range(2)]
    ready = {(u, 1): 2.0 * u[0] for u in units}
    events, now = [], 0.0
    pending = {(u, h) for u in units for h in range(1, 5)}
    arrived = {}
    while pending:
        can = [k for k in pending if k in ready and ready[k] <= now + 1e-9]
        if not can:
            now = min(ready[k] for k in pending if k in ready)
            continue
        pick = min(can, key=lambda k: (units.index(k[0]), k[1]))
        pending.remove(pick)
        events.append((now, "hop", pick[0], pick[1]))
        now += hop_us * (0.5 if pick[1] == 4 else 1.0)
        unit, hop = pick
        if hop < 4:
            ready[(unit, hop + 1)] = now + latency
        else:
            arrived[unit] = now + latency
    start = arrived[(0, 0)]
    events.append((start, "edge", None, None))
    events.append((start + 4.5, "solve1", None, None))
    events.append((start + 8.5, "narrow1", None, None))
    last = start + 11.5
    for c in range(CHUNKS):
        last = max(last, arrived[(c, 0)], arrived[(c, 1)])
        events.append((last, "chunk", c, None))
        last += 0.8
    events.sort(key=lambda e: e[0])
    return events


def kernel(
    x_hbm, f_hbm, d_hbm, sol_ref, upd_ref,
    x_v, f_v, f_wide, f_cut, d_v, buf, nar, low, edge_out, edge_in, back_out, back_in,
    in_sem, own_sem, ysend, yrecv, zsend, zrecv, rsend, rrecv, nsend, nrecv, esend, erecv, bsend, brecv,
):
    row = lax.axis_index("row")
    col = lax.axis_index("col")
    y = col // NZ
    z = col % NZ
    up, down = (z + 1) % NZ, (z + NZ - 1) % NZ

    def at(row_, y_, z_):
        return (row_, y_ * NZ + z_)

    def remote(src, dst, send, recv, device):
        return pltpu.make_async_remote_copy(
            src_ref=src, dst_ref=dst, send_sem=send, recv_sem=recv,
            device_id=device, device_id_type=pl.DeviceIdType.MESH,
        )

    f_in = pltpu.make_async_copy(f_hbm, f_v, in_sem.at[0])
    x_in = pltpu.make_async_copy(x_hbm, x_v, in_sem.at[1])
    d_in = pltpu.make_async_copy(d_hbm, d_v, in_sem.at[2])
    f_in.start()
    x_in.start()
    d_in.start()

    barrier = pltpu.get_barrier_semaphore()
    peers = [at(row, y, up), at(row, y, down)]
    peers += [at(row, (y + d) % NY, z) for d in range(1, NY)]
    peers += [at((row + d) % NROW, y, z) for d in range(1, NROW)]
    for peer in peers:
        pl.semaphore_signal(barrier, inc=1, device_id=peer, device_id_type=pl.DeviceIdType.MESH)

    f_in.wait()
    for l in range(4):
        f_wide[l] = f_v[:, l * 128:(l + 1) * 128].astype(F32)
    own = []
    for c in range(CHUNKS):
        for q in range(NY):
            j = 4 * q + 3 - c
            piece = jnp.concatenate([f_wide[l, pl.ds(j, 32, stride=16), :] for l in range(4)], axis=1)
            f_cut[q, c] = piece.astype(BF16).reshape(2, 16, 512)
        copy = pltpu.make_async_copy(f_cut.at[y, c], buf.at[c, :, y, z], own_sem.at[c])
        copy.start()
        own.append(copy)

    pl.semaphore_wait(barrier, len(peers))

    ycopies = {}
    for c in range(CHUNKS):
        for d in range(1, NY):
            to = (y + d) % NY
            copy = remote(
                f_cut.at[to, c], buf.at[c, :, y, z], ysend.at[c, d - 1], yrecv.at[c, d - 1], at(row, to, z)
            )
            copy.start()
            ycopies[c, d] = copy

    def block_of_rhs(j):
        return jnp.concatenate(
            [x_v[pl.ds(4 * j + l, 64, stride=64), :] for l in range(4)], axis=1
        )

    def spread_row(s, value, root):
        high = value.astype(BF16)
        nar[s, y] = high
        low[s] = (value - high.astype(F32)).astype(BF16)
        for part in range(2):
            for t in range(NROW):
                if t != root:
                    row_copy(s, part, t).start()

    def row_copy(s, part, t):
        ref = nar.at[s, y] if part == 0 else low.at[s]
        return remote(ref, ref, rsend.at[s, part, t], rrecv.at[s, part], at(t, y, z))

    def narrow_copy(s, d):
        ref = nar.at[s, y]
        return remote(ref, ref, nsend.at[s, d - 1], nrecv.at[s, d - 1], at(row, (y + d) % NY, z))

    def share_narrow(s, root):
        @pl.when(row != root)
        def _():
            row_copy(s, 0, 0).wait_recv()

        for d in range(1, NY):
            narrow_copy(s, d).start()

    def store_solved(s, root):
        @pl.when(row != root)
        def _():
            row_copy(s, 1, 0).wait_recv()

        sol_ref[s] = nar[s, y].astype(F32) + low[s].astype(F32)

    x_in.wait()
    d_in.wait()

    @pl.when(row == NROW - 1)
    def _():
        spread_row(
            0,
            jnp.dot(block_of_rhs(15), d_v[0], precision=lax.Precision.HIGHEST, preferred_element_type=F32),
            NROW - 1,
        )

    def hop_copy(unit, hop, way):
        c, s = unit
        n = c * 2 + s
        block = (z - (hop - 1) + NZ) % NZ if way == 0 else (z + hop - 1) % NZ
        if hop < 4:
            ref = buf.at[c, s, :, block]
        else:
            ref = buf.at[c, s, pl.ds(2 * way, 2), block]
        return remote(
            ref, ref, zsend.at[way, n, hop - 1], zrecv.at[way, n, hop - 1],
            at(row, y, up if way == 0 else down),
        )

    def matmul(c, s):
        return jnp.dot(
            nar[s].reshape(256, 512), buf[c, s].reshape(512, 512), preferred_element_type=F32
        )

    def edge_copy(d):
        to = (y + d) % NY
        return remote(edge_out.at[to], edge_in, esend.at[d - 1], erecv.at[0], at(row, to, z))

    def back_copy(c, d):
        to = (y + d) % NY
        return remote(
            back_out.at[c, to], back_in.at[c, y], bsend.at[c, d - 1], brecv.at[c, d - 1], at(row, to, z)
        )

    is_edge = jnp.logical_and(row == NROW - 2, y == NY - 1)
    waited = set()

    def wait_last(unit):
        for way in range(2):
            hop_copy(unit, 4, way).wait_recv()
        waited.add(unit)

    shared0 = False
    for _, kind, what, hop in ring_order():
        if kind == "hop":
            unit = what
            if hop == 1:
                if unit[1] == 0:
                    own[unit[0]].wait()
                    for d in range(1, NY):
                        ycopies[unit[0], d].wait_recv()
                for way in range(2):
                    hop_copy(unit, 1, way).start()
            else:
                if hop == 4 and not shared0:
                    share_narrow(0, NROW - 1)
                    shared0 = True
                for way in range(2):
                    hop_copy(unit, hop - 1, way).wait_recv()
                    hop_copy(unit, hop, way).start()
        elif kind == "edge":
            wait_last((0, 0))
            for d in range(1, NY):
                narrow_copy(0, d).wait_recv()

            @pl.when(is_edge)
            def _():
                edge_out[...] = matmul(0, 0).reshape(NY, 64, 512)
                for d in range(1, NY):
                    edge_copy(d).start()
                edge_in[...] = edge_out[NY - 1]

        elif kind == "solve1":

            @pl.when(row == NROW - 2)
            def _():
                @pl.when(y != NY - 1)
                def _():
                    edge_copy(1).wait_recv()

                spread_row(
                    1,
                    jnp.dot(
                        block_of_rhs(15) - edge_in[...], d_v[1],
                        precision=lax.Precision.HIGHEST, preferred_element_type=F32,
                    ),
                    NROW - 2,
                )

        elif kind == "narrow1":
            share_narrow(1, NROW - 2)
            store_solved(0, NROW - 1)
        else:
            c = what
            if c == 0:
                for d in range(1, NY):
                    narrow_copy(1, d).wait_recv()
            for s in range(2):
                if (c, s) not in waited:
                    wait_last((c, s))
            change = (matmul(c, 0) + matmul(c, 1)).astype(BF16).reshape(NY, 64, 512)
            back_out[c] = change
            for d in range(1, NY):
                back_copy(c, d).start()
            back_in[c, y] = back_out[c, y]

    store_solved(1, NROW - 2)
    for c in range(CHUNKS):
        for d in range(1, NY):
            back_copy(c, d).wait_recv()
        for q in range(NY):
            j = 4 * q + 3 - c

            def finish(change, j=j):
                for l in range(4):
                    rows = pl.ds(4 * j + l, 64, stride=64)
                    upd_ref[rows, :] = x_v[rows, :] - change[:, l * 128:(l + 1) * 128].astype(F32)

            if j < 15:
                finish(back_in[c, q])
            else:
                @pl.when(row < NROW - 2)
                def _():
                    finish(back_in[c, q])

                @pl.when(row == NROW - 2)
                def _():
                    finish(edge_in[...])

                @pl.when(row == NROW - 1)
                def _():
                    finish(jnp.zeros((64, 512), F32))

    for c in range(CHUNKS):
        for d in range(1, NY):
            ycopies[c, d].wait_send()
            back_copy(c, d).wait_send()
        for s in range(2):
            for hop in range(1, 5):
                for way in range(2):
                    hop_copy((c, s), hop, way).wait_send()
    for s in range(2):
        for d in range(1, NY):
            narrow_copy(s, d).wait_send()
    for s in range(2):
        root = NROW - 1 - s

        @pl.when(row == root)
        def _():
            for part in range(2):
                for t in range(NROW):
                    if t != root:
                        row_copy(s, part, t).wait_send()

    @pl.when(is_edge)
    def _():
        for d in range(1, NY):
            edge_copy(d).wait_send()


def on_device(rhs, factor_rows, diag_inverse):
    dma = pltpu.SemaphoreType.DMA
    any_space = pl.BlockSpec(memory_space=pl.ANY)
    solved, updated = pl.pallas_call(
        kernel,
        out_shape=(
            jax.ShapeDtypeStruct((2, 64, 512), F32),
            jax.ShapeDtypeStruct((4096, 128), F32),
        ),
        in_specs=[any_space] * 3,
        out_specs=[pl.BlockSpec(memory_space=pltpu.VMEM)] * 2,
        scratch_shapes=[
            pltpu.VMEM((4096, 128), F32),
            pltpu.VMEM((512, 512), BF16),
            pltpu.VMEM((4, 512, 128), F32),
            pltpu.VMEM((NY, CHUNKS, 2, 16, 512), BF16),
            pltpu.VMEM((2, 512, 512), F32),
            pltpu.VMEM((CHUNKS, 2, NY, NZ, 16, 512), BF16),
            pltpu.VMEM((2, NY, 64, 512), BF16),
            pltpu.VMEM((2, 64, 512), BF16),
            pltpu.VMEM((NY, 64, 512), F32),
            pltpu.VMEM((64, 512), F32),
            pltpu.VMEM((CHUNKS, NY, 64, 512), BF16),
            pltpu.VMEM((CHUNKS, NY, 64, 512), BF16),
            dma((3,)),
            dma((CHUNKS,)),
            dma((CHUNKS, NY - 1)),
            dma((CHUNKS, NY - 1)),
            dma((2, CHUNKS * 2, 4)),
            dma((2, CHUNKS * 2, 4)),
            dma((2, 2, NROW)),
            dma((2, 2)),
            dma((2, NY - 1)),
            dma((2, NY - 1)),
            dma((NY - 1,)),
            dma((1,)),
            dma((CHUNKS, NY - 1)),
            dma((CHUNKS, NY - 1)),
        ],
        compiler_params=pltpu.CompilerParams(
            collective_id=0, has_side_effects=True, vmem_limit_bytes=48 * 1024 * 1024
        ),
        name="back_substitution",
    )(
        rhs.reshape(4096, 128),
        factor_rows.reshape(512, 512),
        diag_inverse,
    )
    return solved, updated.reshape(rhs.shape)


def solution(mesh):
    return jax.shard_map(
        on_device,
        mesh=mesh,
        in_specs=(P("col", None, "row", None), P(None, "col", None, "row", None), P()),
        out_specs=(P(None, "col", None), P("col", None, "row", None)),
        check_vma=False,
    )
```

```python
import functools

import jax
import jax.numpy as jnp
from jax import lax
from jax.experimental import pallas as pl
from jax.experimental.pallas import tpu as pltpu
from jax.sharding import PartitionSpec as P

NY, NZ, NROW = 4, 8, 8
CHUNKS = 4
UNITS = "ABCDEFGH"
ROW_TARGETS = (2, 3, 0, 1, 4, 5, 6, 7)
BF16, F32 = jnp.bfloat16, jnp.float32
ORDER = (
    "A1", "B1", "C1", "A2", "E1", "D1", "A3", "B2", "F1", "A4", "G1",
    "C2", "B3", "H1", "edge", "C3", "D2", "B4", "F2", "E2", "C4", "solve",
    "D3", "F3", "G2", "share", "E3", "D4", "F4", "H2", "c0", "E4", "G3",
    "c1", "H3", "c2", "G4", "H4", "f0", "f1", "c3", "f2", "f3",
)


def kernel(
    x_hbm, f_hbm, d_hbm, sol_ref, upd_ref,
    x_v, f_v, f_wide, f_cut, d_v, d_cut, buf, nar, lhs, low, edge_out, edge_in, back_out, back_in,
    in_sem, own_sem, ysend, yrecv, osend, orecv, zsend, zrecv, rsend, rrecv, nsend, nrecv,
    esend, erecv, bsend, brecv,
):
    row = lax.axis_index("row")
    col = lax.axis_index("col")
    y = col // NZ
    z = col % NZ
    up, down = (z + 1) % NZ, (z + NZ - 1) % NZ
    first_root, second_root = NROW - 1, NROW - 2

    def at(row_, y_, z_):
        return (row_, y_ * NZ + z_)

    def remote(src, dst, send, recv, device):
        return pltpu.make_async_remote_copy(
            src_ref=src, dst_ref=dst, send_sem=send, recv_sem=recv,
            device_id=device, device_id_type=pl.DeviceIdType.MESH,
        )

    def signal(device):
        pl.semaphore_signal(barrier, inc=1, device_id=device, device_id_type=pl.DeviceIdType.MESH)

    barrier = pltpu.get_barrier_semaphore()
    signal(at(row, y, up))
    signal(at(row, y, down))
    for d in range(1, NY):
        signal(at(row, (y + d) % NY, z))
    for root in (first_root, second_root):
        for t in range(NROW):
            if t != root:
                if t < second_root:
                    @pl.when(row == root)
                    def _(t=t):
                        signal(at(t, y, z))

                    @pl.when(row == t)
                    def _(root=root):
                        signal(at(root, y, z))
                else:
                    @pl.when(row == root)
                    def _(t=t):
                        signal(at(t, y, z))

    f_in = pltpu.make_async_copy(f_hbm, f_v, in_sem.at[0])
    x_in = pltpu.make_async_copy(x_hbm, x_v, in_sem.at[1])
    d_in = pltpu.make_async_copy(d_hbm.at[jnp.where(row == first_root, 0, 1)], d_v, in_sem.at[2])
    f_in.start()
    d_in.start()
    x_in.start()

    f_in.wait()
    for l in range(4):
        f_wide[l] = f_v[:, l * 128:(l + 1) * 128].astype(F32)
    for c in range(CHUNKS):
        for q in range(NY):
            j = 4 * q + 3 - c
            piece = jnp.concatenate([f_wide[l, pl.ds(j, 32, stride=16), :] for l in range(4)], axis=1)
            f_cut[q, c] = piece.astype(BF16).reshape(2, 16, 512)
    own = pltpu.make_async_copy(f_cut.at[y], buf.at[:, :, 0, z], own_sem)
    own.start()

    @pl.when(row >= second_root)
    def _():
        pl.semaphore_wait(barrier, 2 + NY - 1 + NROW - 1)

    @pl.when(row < second_root)
    def _():
        pl.semaphore_wait(barrier, 2 + NY - 1 + 2)

    def y_copy(c, d):
        to = (y + d) % NY
        return remote(
            f_cut.at[to, c], buf.at[c, :, NY - d, z], ysend.at[c, d - 1], yrecv.at[c, d - 1], at(row, to, z)
        )

    def own_copy(part, way):
        chunks = pl.ds(0, 1) if part == 0 else pl.ds(1, CHUNKS - 1)
        return remote(
            f_cut.at[y, chunks], buf.at[chunks, :, 0, z], osend.at[part, way], orecv.at[part, way],
            at(row, y, up if way == 0 else down),
        )

    for c in range(CHUNKS):
        for d in range(1, NY):
            y_copy(c, d).start()
        if c < 2:
            for way in range(2):
                own_copy(c, way).start()

    def block_of_rhs(j):
        return jnp.concatenate(
            [x_v[pl.ds(4 * j + l, 64, stride=64), :] for l in range(4)], axis=1
        )

    def halves(value):
        high = value.astype(BF16)
        return high, (value - high.astype(F32)).astype(BF16)

    def times_inverse(value):
        high, rest = halves(value)
        dot = functools.partial(jnp.dot, preferred_element_type=F32)
        return dot(high, d_cut[0]) + (dot(high, d_cut[1]) + dot(rest, d_cut[0]))

    def spread_row(s, value, root):
        nar[s, y], low[s] = halves(value)
        for part in range(2):
            for t in ROW_TARGETS:
                if t != root:
                    row_copy(s, part, t).start()

    def row_copy(s, part, t):
        ref = nar.at[s, y] if part == 0 else low.at[s]
        return remote(ref, ref, rsend.at[s, part, t], rrecv.at[s, part], at(t, y, z))

    def narrow_copy(s, d):
        ref = nar.at[s, y]
        return remote(ref, ref, nsend.at[s, d - 1], nrecv.at[s, d - 1], at(row, (y + d) % NY, z))

    def share_narrow(s, root):
        @pl.when(row != root)
        def _():
            row_copy(s, 0, 0).wait_recv()

        for d in range(1, NY):
            narrow_copy(s, d).start()

    def take_narrow(s):
        for d in range(1, NY):
            narrow_copy(s, d).wait_recv()
        for d in range(NY):
            columns = pl.ds(pl.multiple_of((y + d) % NY * 128, 128), 128)
            for q in range(NY):
                lhs[q * 64:(q + 1) * 64, s * 512 + d * 128:s * 512 + (d + 1) * 128] = nar[s, q, :, columns]

    def store_solved(s, root):
        @pl.when(row != root)
        def _():
            row_copy(s, 1, 0).wait_recv()

        sol_ref[s] = nar[s, y].astype(F32) + low[s].astype(F32)

    d_in.wait()
    x_in.wait()

    @pl.when(row >= second_root)
    def _():
        for i in range(4):
            rows = slice(i * 128, (i + 1) * 128)
            d_cut[0, rows], d_cut[1, rows] = halves(d_v[rows])

    @pl.when(row == first_root)
    def _():
        spread_row(0, times_inverse(block_of_rhs(15)), first_root)

    def hop_copy(unit, hop, way):
        c, s = unit
        n = c * 2 + s
        block = (z - (hop - 1) + NZ) % NZ if way == 0 else (z + hop - 1) % NZ
        if hop == 1:
            ref = buf.at[c, s, pl.ds(1, NY - 1), block]
        elif hop < 4:
            ref = buf.at[c, s, :, block]
        else:
            ref = buf.at[c, s, pl.ds(2 * way, 2), block]
        return remote(
            ref, ref, zsend.at[way, n, hop - 1], zrecv.at[way, n, hop - 1],
            at(row, y, up if way == 0 else down),
        )

    def edge_copy(d):
        to = (y + d) % NY
        return remote(edge_out.at[to], edge_in, esend.at[d - 1], erecv.at[0], at(row, to, z))

    def back_copy(c, d):
        to = (y + d) % NY
        return remote(
            back_out.at[c, to], back_in.at[c, y], bsend.at[c, d - 1], brecv.at[c, d - 1], at(row, to, z)
        )

    is_edge = jnp.logical_and(row == second_root, y == NY - 1)

    def wait_last(unit):
        for way in range(2):
            hop_copy(unit, 4, way).wait_recv()

    def subtract(j, change):
        for l in range(4):
            rows = pl.ds(4 * j + l, 64, stride=64)
            upd_ref[rows, :] = x_v[rows, :] - change[:, l * 128:(l + 1) * 128].astype(F32)

    own_seen, y_seen = set(), set()
    own.wait()
    for step in ORDER:
        if step[0] in UNITS and len(step) == 2:
            n = UNITS.index(step[0])
            unit, hop = (n // 2, n % 2), int(step[1])
            c = unit[0]
            if hop == 1 and c not in y_seen:
                y_seen.add(c)
                for d in range(1, NY):
                    y_copy(c, d).wait_recv()
            if hop == 2 and min(c, 1) not in own_seen:
                own_seen.add(min(c, 1))
                for way in range(2):
                    own_copy(min(c, 1), way).wait_recv()
            if step == "A3":
                share_narrow(0, first_root)
            for way in range(2):
                if hop > 1:
                    hop_copy(unit, hop - 1, way).wait_recv()
                hop_copy(unit, hop, way).start()
        elif step == "edge":
            take_narrow(0)
            wait_last((0, 0))

            @pl.when(is_edge)
            def _():
                product = jnp.dot(
                    lhs[:, :512], buf[0, 0].reshape(512, 512), preferred_element_type=F32
                )
                edge_out[...] = product.reshape(NY, 64, 512)
                for d in range(1, NY):
                    edge_copy(d).start()
                edge_in[...] = edge_out[NY - 1]

            store_solved(0, first_root)

        elif step == "solve":

            @pl.when(row == second_root)
            def _():
                @pl.when(y != NY - 1)
                def _():
                    edge_copy(1).wait_recv()

                spread_row(1, times_inverse(block_of_rhs(15) - edge_in[...]), second_root)

        elif step == "share":
            share_narrow(1, second_root)
        elif step[0] == "c":
            c = int(step[1])
            if c == 0:
                take_narrow(1)
            for s in range(2):
                if (c, s) != (0, 0):
                    wait_last((c, s))
            change = jnp.dot(lhs[...], buf[c].reshape(1024, 512), preferred_element_type=F32)
            back_out[c] = change.astype(BF16).reshape(NY, 64, 512)
            for d in range(1, NY):
                back_copy(c, d).start()
            back_in[c, y] = back_out[c, y]
        else:
            c = int(step[1])
            if c == 0:
                store_solved(1, second_root)
            for d in range(1, NY):
                back_copy(c, d).wait_recv()
            for q in range(NY):
                j = 4 * q + 3 - c
                if j < 15:
                    subtract(j, back_in[c, q])
                else:
                    @pl.when(row < second_root)
                    def _():
                        subtract(15, back_in[0, NY - 1])

                    @pl.when(row == second_root)
                    def _():
                        subtract(15, edge_in[...])

                    @pl.when(row == first_root)
                    def _():
                        subtract(15, jnp.zeros((64, 512), F32))

    for c in range(CHUNKS):
        for d in range(1, NY):
            y_copy(c, d).wait_send()
            back_copy(c, d).wait_send()
        for s in range(2):
            for hop in range(1, 5):
                for way in range(2):
                    hop_copy((c, s), hop, way).wait_send()
    for part in range(2):
        for way in range(2):
            own_copy(part, way).wait_send()
    for s in range(2):
        for d in range(1, NY):
            narrow_copy(s, d).wait_send()
    for s in range(2):
        root = NROW - 1 - s

        @pl.when(row == root)
        def _():
            for part in range(2):
                for t in range(NROW):
                    if t != root:
                        row_copy(s, part, t).wait_send()

    @pl.when(is_edge)
    def _():
        for d in range(1, NY):
            edge_copy(d).wait_send()


def on_device(rhs, factor_rows, diag_inverse):
    dma = pltpu.SemaphoreType.DMA
    any_space = pl.BlockSpec(memory_space=pl.ANY)
    in_hbm = functools.partial(pltpu.with_memory_space_constraint, memory_space=pltpu.HBM)
    solved, updated = pl.pallas_call(
        kernel,
        out_shape=(
            pltpu.VMEM((2, 64, 512), F32),
            pltpu.VMEM((4096, 128), F32),
        ),
        in_specs=[any_space] * 3,
        out_specs=[pl.BlockSpec(memory_space=pltpu.VMEM)] * 2,
        scratch_shapes=[
            pltpu.VMEM((4096, 128), F32),
            pltpu.VMEM((512, 512), BF16),
            pltpu.VMEM((4, 512, 128), F32),
            pltpu.VMEM((NY, CHUNKS, 2, 16, 512), BF16),
            pltpu.VMEM((512, 512), F32),
            pltpu.VMEM((2, 512, 512), BF16),
            pltpu.VMEM((CHUNKS, 2, NY, NZ, 16, 512), BF16),
            pltpu.VMEM((2, NY, 64, 512), BF16),
            pltpu.VMEM((256, 1024), BF16),
            pltpu.VMEM((2, 64, 512), BF16),
            pltpu.VMEM((NY, 64, 512), F32),
            pltpu.VMEM((64, 512), F32),
            pltpu.VMEM((CHUNKS, NY, 64, 512), BF16),
            pltpu.VMEM((CHUNKS, NY, 64, 512), BF16),
            dma((3,)),
            dma,
            dma((CHUNKS, NY - 1)),
            dma((CHUNKS, NY - 1)),
            dma((2, 2)),
            dma((2, 2)),
            dma((2, CHUNKS * 2, 4)),
            dma((2, CHUNKS * 2, 4)),
            dma((2, 2, NROW)),
            dma((2, 2)),
            dma((2, NY - 1)),
            dma((2, NY - 1)),
            dma((NY - 1,)),
            dma((1,)),
            dma((CHUNKS, NY - 1)),
            dma((CHUNKS, NY - 1)),
        ],
        compiler_params=pltpu.CompilerParams(
            collective_id=0, has_side_effects=True, vmem_limit_bytes=48 * 1024 * 1024
        ),
        name="back_substitution",
    )(
        in_hbm(rhs.reshape(4096, 128)),
        in_hbm(factor_rows.reshape(512, 512)),
        in_hbm(diag_inverse),
    )
    return solved, updated.reshape(rhs.shape)


def solution(mesh):
    return jax.shard_map(
        on_device,
        mesh=mesh,
        in_specs=(P("col", None, "row", None), P(None, "col", None, "row", None), P()),
        out_specs=(P(None, "col", None), P("col", None, "row", None)),
        check_vma=False,
    )
```

```python
import functools

import jax
import jax.numpy as jnp
from jax import lax
from jax.experimental import pallas as pl
from jax.experimental.pallas import tpu as pltpu
from jax.sharding import PartitionSpec as P

NY, NZ, NROW = 4, 8, 8
CHUNKS = 4
UNITS = "ABCDEFGH"
ROW_TARGETS = (6, 2, 3, 0, 1, 4, 5, 7)
FAR = (2, 3, 4, 5, 6)
BF16, F32 = jnp.bfloat16, jnp.float32
BOUNDS = (0, 5, 10, 14, 16)
ORDER = (
    "A1", "B1", "C1", "e0", "G1", "D1", "e1", "H1", "C2", "D2", "edge",
    "G2", "B2", "E1", "A2", "D3", "F1", "B3", "C3", "solve", "D4", "A3",
    "E2", "n0", "F2", "C4", "share", "A4", "B4", "F3", "E3", "H2", "c1",
    "G3", "c0", "F4", "E4", "H3", "G4", "c2", "H4", "c3", "f0", "f1",
    "f2", "f3",
)


def kernel(
    x_hbm, f_hbm, d_hbm, sol_ref, upd_ref,
    x_v, f_v, f_wide, f_cut, d_v, d_cut, buf, edge_f, nar, lhs, low, edge_out, edge_in, back_out, back_in,
    in_sem, own_sem, ysend, yrecv, osend, orecv, zsend, zrecv, rsend, rrecv, nsend, nrecv,
    esend, erecv, pysend, pyrecv, pzsend, pzrecv, bsend, brecv,
):
    row = lax.axis_index("row")
    col = lax.axis_index("col")
    y = col // NZ
    z = col % NZ
    up, down = (z + 1) % NZ, (z + NZ - 1) % NZ
    first_root, second_root = NROW - 1, NROW - 2

    def at(row_, y_, z_):
        return (row_, y_ * NZ + z_)

    def remote(src, dst, send, recv, device):
        return pltpu.make_async_remote_copy(
            src_ref=src, dst_ref=dst, send_sem=send, recv_sem=recv,
            device_id=device, device_id_type=pl.DeviceIdType.MESH,
        )

    def signal(device):
        pl.semaphore_signal(barrier, inc=1, device_id=device, device_id_type=pl.DeviceIdType.MESH)

    barrier = pltpu.get_barrier_semaphore()
    signal(at(row, y, up))
    signal(at(row, y, down))
    for d in range(1, NY):
        signal(at(row, (y + d) % NY, z))
    for root in (first_root, second_root):
        for t in range(NROW):
            if t != root:
                if t < second_root:
                    @pl.when(row == root)
                    def _(t=t):
                        signal(at(t, y, z))

                    @pl.when(row == t)
                    def _(root=root):
                        signal(at(root, y, z))
                else:
                    @pl.when(row == root)
                    def _(t=t):
                        signal(at(t, y, z))

    @pl.when(row == second_root)
    def _():
        for d in FAR:
            signal(at(row, y, (z + d) % NZ))

    f_in = pltpu.make_async_copy(f_hbm, f_v, in_sem.at[0])
    x_in = pltpu.make_async_copy(x_hbm, x_v, in_sem.at[1])
    d_in = pltpu.make_async_copy(d_hbm.at[jnp.where(row == first_root, 0, 1)], d_v, in_sem.at[2])
    f_in.start()
    d_in.start()
    x_in.start()

    f_in.wait()
    for l in range(4):
        f_wide[l] = f_v[:, l * 128:(l + 1) * 128].astype(F32)
    for q in range(NY):
        for j in range(16):
            f_cut[q, j] = f_wide[q, pl.ds(j, 32, stride=16), :].astype(BF16).reshape(2, 16, 128)
    own = pltpu.make_async_copy(f_cut.at[y], buf.at[:, :, 0, z], own_sem)
    own.start()

    def span(c):
        return pl.ds(BOUNDS[c], BOUNDS[c + 1] - BOUNDS[c])

    def y_copy(c, d):
        to = (y + d) % NY
        return remote(
            f_cut.at[to, span(c)], buf.at[span(c), :, NY - d, z],
            ysend.at[c, d - 1], yrecv.at[c, d - 1], at(row, to, z),
        )

    def own_copy(part, way):
        blocks = span(0) if part == 0 else pl.ds(BOUNDS[1], 16 - BOUNDS[1])
        return remote(
            f_cut.at[y, blocks], buf.at[blocks, :, 0, z], osend.at[part, way], orecv.at[part, way],
            at(row, y, up if way == 0 else down),
        )

    def piece_y_copy(d):
        to = (y + d) % NY
        return remote(
            f_cut.at[to, 15, 0], edge_f.at[NY - d, z], pysend.at[d - 1], pyrecv.at[d - 1], at(row, to, z)
        )

    def piece_z_copy(d):
        return remote(
            edge_f.at[:, z], edge_f.at[:, z], pzsend.at[d - 1], pzrecv.at[d - 1], at(row, y, (z + d) % NZ)
        )

    def block_of_rhs(j):
        return jnp.concatenate(
            [x_v[pl.ds(4 * j + l, 64, stride=64), :] for l in range(4)], axis=1
        )

    def halves(value):
        high = value.astype(BF16)
        return high, (value - high.astype(F32)).astype(BF16)

    def times_inverse(value):
        high, rest = halves(value)
        dot = functools.partial(jnp.dot, preferred_element_type=F32)
        return dot(high, d_cut[0]) + (dot(high, d_cut[1]) + dot(rest, d_cut[0]))

    def spread_row(s, root):
        for part in range(2):
            for t in ROW_TARGETS:
                if t != root:
                    row_copy(s, part, t).start()

    def row_copy(s, part, t):
        ref = nar.at[s, y] if part == 0 else low.at[s]
        return remote(ref, ref, rsend.at[s, part, t], rrecv.at[s, part], at(t, y, z))

    def narrow_copy(s, d):
        ref = nar.at[s, y]
        return remote(ref, ref, nsend.at[s, d - 1], nrecv.at[s, d - 1], at(row, (y + d) % NY, z))

    def share_narrow(s, root):
        @pl.when(row != root)
        def _():
            row_copy(s, 0, 0).wait_recv()

        for d in range(1, NY):
            narrow_copy(s, d).start()

    def take_narrow(s):
        for d in range(1, NY):
            narrow_copy(s, d).wait_recv()
        for d in range(NY):
            columns = pl.ds(pl.multiple_of((y + d) % NY * 128, 128), 128)
            for q in range(NY):
                lhs[q * 64:(q + 1) * 64, s * 512 + d * 128:s * 512 + (d + 1) * 128] = nar[s, q, :, columns]

    def store_solved(s, root):
        @pl.when(row != root)
        def _():
            row_copy(s, 1, 0).wait_recv()

        sol_ref[s] = nar[s, y].astype(F32) + low[s].astype(F32)

    d_in.wait()
    x_in.wait()

    @pl.when(row >= second_root)
    def _():
        for i in range(4):
            rows = slice(i * 128, (i + 1) * 128)
            d_cut[0, rows], d_cut[1, rows] = halves(d_v[rows])

    @pl.when(row == first_root)
    def _():
        nar[0, y], low[0] = halves(times_inverse(block_of_rhs(15)))

    @pl.when(row == first_root)
    def _():
        pl.semaphore_wait(barrier, 2 + NY - 1 + NROW - 1)
        spread_row(0, first_root)

    @pl.when(row == second_root)
    def _():
        pl.semaphore_wait(barrier, 2 + NY - 1 + NROW - 1 + len(FAR))
        for d in range(1, NY):
            piece_y_copy(d).start()
        edge_f[0, z] = f_cut[y, 15, 0]

    @pl.when(row < second_root)
    def _():
        pl.semaphore_wait(barrier, 2 + NY - 1 + 2)

    for c in range(CHUNKS):
        for d in range(1, NY):
            y_copy(c, d).start()
        if c < 2:
            for way in range(2):
                own_copy(c, way).start()

    def hop_copy(unit, hop, way):
        c, s = unit
        n = c * 2 + s
        block = (z - (hop - 1) + NZ) % NZ if way == 0 else (z + hop - 1) % NZ
        if hop == 1:
            ref = buf.at[span(c), s, pl.ds(1, NY - 1), block]
        elif hop < 4:
            ref = buf.at[span(c), s, :, block]
        else:
            ref = buf.at[span(c), s, pl.ds(2 * way, 2), block]
        return remote(
            ref, ref, zsend.at[way, n, hop - 1], zrecv.at[way, n, hop - 1],
            at(row, y, up if way == 0 else down),
        )

    def edge_copy(d):
        to = (y + d) % NY
        return remote(edge_out.at[to], edge_in.at[y], esend.at[d - 1], erecv.at[d - 1], at(row, to, z))

    def back_copy(c, d):
        to = (y + d) % NY
        return remote(
            back_out.at[to, span(c)], back_in.at[y, span(c)], bsend.at[c, d - 1], brecv.at[c, d - 1], at(row, to, z)
        )

    def wait_last(unit):
        for way in range(2):
            hop_copy(unit, 4, way).wait_recv()

    def subtract(j, q, change):
        rows = pl.ds(4 * j + q, 64, stride=64)
        upd_ref[rows, :] = x_v[rows, :] - change.astype(F32)

    own_seen, y_seen = set(), set()
    multiplied = stored = False
    own.wait()
    for step in ORDER:
        if step[0] in UNITS and len(step) == 2:
            n = UNITS.index(step[0])
            unit, hop = (n // 2, n % 2), int(step[1])
            c = unit[0]
            if hop == 1 and c not in y_seen:
                y_seen.add(c)
                for d in range(1, NY):
                    y_copy(c, d).wait_recv()
            if hop == 2 and min(c, 1) not in own_seen:
                own_seen.add(min(c, 1))
                for way in range(2):
                    own_copy(min(c, 1), way).wait_recv()
            for way in range(2):
                if hop > 1:
                    hop_copy(unit, hop - 1, way).wait_recv()
                hop_copy(unit, hop, way).start()
        elif step == "e0":

            @pl.when(row >= second_root)
            def _():
                share_narrow(0, first_root)

        elif step == "e1":

            @pl.when(row == second_root)
            def _():
                for d in range(1, NY):
                    piece_y_copy(d).wait_recv()
                for d in range(1, NZ):
                    piece_z_copy(d).start()

        elif step == "n0":

            @pl.when(row < second_root)
            def _():
                share_narrow(0, first_root)

        elif step == "edge":

            @pl.when(row == second_root)
            def _():
                take_narrow(0)
                for d in range(1, NZ):
                    piece_z_copy(d).wait_recv()
                product = jnp.dot(
                    lhs[:, :512], edge_f[...].reshape(512, 128), preferred_element_type=F32
                )
                edge_out[...] = product.reshape(NY, 64, 128)
                for d in range(1, NY):
                    edge_copy(d).start()
                edge_in[y] = edge_out[y]

        elif step == "solve":

            @pl.when(row == second_root)
            def _():
                for d in range(1, NY):
                    edge_copy(d).wait_recv()
                change = jnp.concatenate([edge_in[q] for q in range(NY)], axis=1)
                nar[1, y], low[1] = halves(times_inverse(block_of_rhs(15) - change))
                spread_row(1, second_root)

        elif step == "share":
            share_narrow(1, second_root)
        elif step[0] == "c":
            c = int(step[1])
            if not multiplied:
                multiplied = True

                @pl.when(row != second_root)
                def _():
                    take_narrow(0)

                take_narrow(1)
            for s in range(2):
                wait_last((c, s))
            for j in range(BOUNDS[c], BOUNDS[c + 1], 2):
                width = min(2, BOUNDS[c + 1] - j)
                factor = jnp.concatenate([buf[j + i].reshape(1024, 128) for i in range(width)], axis=1)
                change = jnp.dot(lhs[...], factor, preferred_element_type=F32).astype(BF16)
                for i in range(width):
                    back_out[:, j + i] = change[:, i * 128:(i + 1) * 128].reshape(NY, 64, 128)
            for d in range(1, NY):
                back_copy(c, d).start()
        else:
            c = int(step[1])
            if not stored:
                stored = True
                for s in range(2):
                    store_solved(s, NROW - 1 - s)
            for d in range(1, NY):
                back_copy(c, d).wait_recv()
            back_in[y, span(c)] = back_out[y, span(c)]
            for q in range(NY):
                for j in range(BOUNDS[c], BOUNDS[c + 1]):
                    if j < 15:
                        subtract(j, q, back_in[q, j])
                    else:
                        @pl.when(row < second_root)
                        def _(q=q):
                            subtract(15, q, back_in[q, 15])

                        @pl.when(row == second_root)
                        def _(q=q):
                            subtract(15, q, edge_in[q])

                        @pl.when(row == first_root)
                        def _(q=q):
                            subtract(15, q, jnp.zeros((64, 128), F32))

    for c in range(CHUNKS):
        for d in range(1, NY):
            y_copy(c, d).wait_send()
            back_copy(c, d).wait_send()
        for s in range(2):
            for hop in range(1, 5):
                for way in range(2):
                    hop_copy((c, s), hop, way).wait_send()
    for part in range(2):
        for way in range(2):
            own_copy(part, way).wait_send()
    for s in range(2):
        for d in range(1, NY):
            narrow_copy(s, d).wait_send()
    for s in range(2):
        root = NROW - 1 - s

        @pl.when(row == root)
        def _():
            for part in range(2):
                for t in range(NROW):
                    if t != root:
                        row_copy(s, part, t).wait_send()

    @pl.when(row == second_root)
    def _():
        for d in range(1, NY):
            piece_y_copy(d).wait_send()
            edge_copy(d).wait_send()
        for d in range(1, NZ):
            piece_z_copy(d).wait_send()


def on_device(rhs, factor_rows, diag_inverse):
    dma = pltpu.SemaphoreType.DMA
    any_space = pl.BlockSpec(memory_space=pl.ANY)
    in_hbm = functools.partial(pltpu.with_memory_space_constraint, memory_space=pltpu.HBM)
    solved, updated = pl.pallas_call(
        kernel,
        out_shape=(
            pltpu.VMEM((2, 64, 512), F32),
            pltpu.VMEM((4096, 128), F32),
        ),
        in_specs=[any_space] * 3,
        out_specs=[pl.BlockSpec(memory_space=pltpu.VMEM)] * 2,
        scratch_shapes=[
            pltpu.VMEM((4096, 128), F32),
            pltpu.VMEM((512, 512), BF16),
            pltpu.VMEM((4, 512, 128), F32),
            pltpu.VMEM((NY, 16, 2, 16, 128), BF16),
            pltpu.VMEM((512, 512), F32),
            pltpu.VMEM((2, 512, 512), BF16),
            pltpu.VMEM((16, 2, NY, NZ, 16, 128), BF16),
            pltpu.VMEM((NY, NZ, 16, 128), BF16),
            pltpu.VMEM((2, NY, 64, 512), BF16),
            pltpu.VMEM((256, 1024), BF16),
            pltpu.VMEM((2, 64, 512), BF16),
            pltpu.VMEM((NY, 64, 128), F32),
            pltpu.VMEM((NY, 64, 128), F32),
            pltpu.VMEM((NY, 16, 64, 128), BF16),
            pltpu.VMEM((NY, 16, 64, 128), BF16),
            dma((3,)),
            dma,
            dma((CHUNKS, NY - 1)),
            dma((CHUNKS, NY - 1)),
            dma((2, 2)),
            dma((2, 2)),
            dma((2, CHUNKS * 2, 4)),
            dma((2, CHUNKS * 2, 4)),
            dma((2, 2, NROW)),
            dma((2, 2)),
            dma((2, NY - 1)),
            dma((2, NY - 1)),
            dma((NY - 1,)),
            dma((NY - 1,)),
            dma((NY - 1,)),
            dma((NY - 1,)),
            dma((NZ - 1,)),
            dma((NZ - 1,)),
            dma((CHUNKS, NY - 1)),
            dma((CHUNKS, NY - 1)),
        ],
        compiler_params=pltpu.CompilerParams(
            collective_id=0, has_side_effects=True, vmem_limit_bytes=48 * 1024 * 1024
        ),
        name="back_substitution",
    )(
        in_hbm(rhs.reshape(4096, 128)),
        in_hbm(factor_rows.reshape(512, 512)),
        in_hbm(diag_inverse),
    )
    return solved, updated.reshape(rhs.shape)


def solution(mesh):
    return jax.shard_map(
        on_device,
        mesh=mesh,
        in_specs=(P("col", None, "row", None), P(None, "col", None, "row", None), P()),
        out_specs=(P(None, "col", None), P("col", None, "row", None)),
        check_vma=False,
    )
```

```python
import functools

import jax
import jax.numpy as jnp
from jax import lax
from jax.experimental import pallas as pl
from jax.experimental.pallas import tpu as pltpu
from jax.sharding import PartitionSpec as P

NY, NZ, NROW = 4, 8, 8
CHUNKS = 4
UNITS = "ABCDEFGH"
ROW_TARGETS = (6, 2, 3, 0, 1, 4, 5, 7)
FAR = (2, 3, 4, 5, 6)
BF16, F32 = jnp.bfloat16, jnp.float32
BOUNDS = (0, 5, 10, 14, 16)
ORDER = (
    "e1", "A1", "B1", "e0", "D1", "A2", "G1", "H1", "E1", "B2", "C1",
    "n0", "A3", "D2", "edge", "C2", "A4", "E2", "solve", "B3", "F1", "C3",
    "D3", "share", "B4", "G2", "F2", "D4", "H2", "C4", "E3", "c0", "F3",
    "H3", "G3", "c1", "E4", "F4", "H4", "G4", "c2", "c3", "f0", "f1",
    "f2", "f3",
)


def kernel(
    x_hbm, f_hbm, d_hbm, sol_ref, upd_ref,
    x_v, f_v, f_wide, f_cut, d_v, d_cut, buf, edge_f, nar, lhs, low, edge_out, edge_in, back_out, back_in,
    in_sem, own_sem, ysend, yrecv, osend, orecv, zsend, zrecv, rsend, rrecv, nsend, nrecv,
    esend, erecv, pysend, pyrecv, pzsend, pzrecv, bsend, brecv,
):
    row = lax.axis_index("row")
    col = lax.axis_index("col")
    y = col // NZ
    z = col % NZ
    up, down = (z + 1) % NZ, (z + NZ - 1) % NZ
    first_root, second_root = NROW - 1, NROW - 2

    def at(row_, y_, z_):
        return (row_, y_ * NZ + z_)

    def remote(src, dst, send, recv, device):
        return pltpu.make_async_remote_copy(
            src_ref=src, dst_ref=dst, send_sem=send, recv_sem=recv,
            device_id=device, device_id_type=pl.DeviceIdType.MESH,
        )

    def signal(device):
        pl.semaphore_signal(barrier, inc=1, device_id=device, device_id_type=pl.DeviceIdType.MESH)

    barrier = pltpu.get_barrier_semaphore()
    signal(at(row, y, up))
    signal(at(row, y, down))
    for d in range(1, NY):
        signal(at(row, (y + d) % NY, z))
    for root in (first_root, second_root):
        for t in range(NROW):
            if t != root:
                if t < second_root:
                    @pl.when(row == root)
                    def _(t=t):
                        signal(at(t, y, z))

                    @pl.when(row == t)
                    def _(root=root):
                        signal(at(root, y, z))
                else:
                    @pl.when(row == root)
                    def _(t=t):
                        signal(at(t, y, z))

    @pl.when(row == second_root)
    def _():
        for d in FAR:
            signal(at(row, y, (z + d) % NZ))

    f_in = pltpu.make_async_copy(f_hbm, f_v, in_sem.at[0])
    x_in = pltpu.make_async_copy(x_hbm, x_v, in_sem.at[1])
    d_in = pltpu.make_async_copy(d_hbm.at[jnp.where(row == first_root, 0, 1)], d_v, in_sem.at[2])
    f_in.start()
    d_in.start()
    x_in.start()

    f_in.wait()
    for l in range(4):
        f_wide[l] = f_v[:, l * 128:(l + 1) * 128].astype(F32)
    for q in range(NY):
        for j in range(16):
            f_cut[q, j] = f_wide[q, pl.ds(j, 32, stride=16), :].astype(BF16).reshape(2, 16, 128)
    own = pltpu.make_async_copy(f_cut.at[y], buf.at[:, :, 0, z], own_sem)
    own.start()

    def span(c):
        return pl.ds(BOUNDS[c], BOUNDS[c + 1] - BOUNDS[c])

    def y_copy(c, d):
        to = (y + d) % NY
        return remote(
            f_cut.at[to, span(c)], buf.at[span(c), :, NY - d, z],
            ysend.at[c, d - 1], yrecv.at[c, d - 1], at(row, to, z),
        )

    def own_copy(part, way):
        blocks = span(0) if part == 0 else pl.ds(BOUNDS[1], 16 - BOUNDS[1])
        return remote(
            f_cut.at[y, blocks], buf.at[blocks, :, 0, z], osend.at[part, way], orecv.at[part, way],
            at(row, y, up if way == 0 else down),
        )

    def piece_y_copy(d):
        to = (y + d) % NY
        return remote(
            f_cut.at[to, 15, 0], edge_f.at[NY - d, z], pysend.at[d - 1], pyrecv.at[d - 1], at(row, to, z)
        )

    def piece_z_copy(d):
        return remote(
            edge_f.at[:, z], edge_f.at[:, z], pzsend.at[d - 1], pzrecv.at[d - 1], at(row, y, (z + d) % NZ)
        )

    def block_of_rhs(j):
        return jnp.concatenate(
            [x_v[pl.ds(4 * j + l, 64, stride=64), :] for l in range(4)], axis=1
        )

    def halves(value):
        high = value.astype(BF16)
        return high, (value - high.astype(F32)).astype(BF16)

    def times_inverse(value):
        high, rest = halves(value)
        dot = functools.partial(jnp.dot, preferred_element_type=F32)
        return dot(high, d_cut[0]) + (dot(high, d_cut[1]) + dot(rest, d_cut[0]))

    def spread_row(s, root):
        for part in range(2):
            for t in ROW_TARGETS:
                if t != root:
                    row_copy(s, part, t).start()

    def row_copy(s, part, t):
        ref = nar.at[s, y] if part == 0 else low.at[s]
        return remote(ref, ref, rsend.at[s, part, t], rrecv.at[s, part], at(t, y, z))

    def narrow_copy(s, d):
        ref = nar.at[s, y]
        return remote(ref, ref, nsend.at[s, d - 1], nrecv.at[s, d - 1], at(row, (y + d) % NY, z))

    def share_narrow(s, root):
        @pl.when(row != root)
        def _():
            row_copy(s, 0, 0).wait_recv()

        for d in range(1, NY):
            narrow_copy(s, d).start()

    def take_narrow(s):
        for d in range(1, NY):
            narrow_copy(s, d).wait_recv()
        for d in range(NY):
            columns = pl.ds(pl.multiple_of((y + d) % NY * 128, 128), 128)
            for q in range(NY):
                lhs[q * 64:(q + 1) * 64, s * 512 + d * 128:s * 512 + (d + 1) * 128] = nar[s, q, :, columns]

    def store_solved(s, root):
        @pl.when(row != root)
        def _():
            row_copy(s, 1, 0).wait_recv()

        sol_ref[s] = nar[s, y].astype(F32) + low[s].astype(F32)

    d_in.wait()
    x_in.wait()

    @pl.when(row >= second_root)
    def _():
        for i in range(4):
            rows = slice(i * 128, (i + 1) * 128)
            d_cut[0, rows], d_cut[1, rows] = halves(d_v[rows])

    @pl.when(row == first_root)
    def _():
        nar[0, y], low[0] = halves(times_inverse(block_of_rhs(15)))

    @pl.when(row == first_root)
    def _():
        pl.semaphore_wait(barrier, 2 + NY - 1 + NROW - 1)
        spread_row(0, first_root)

    @pl.when(row == second_root)
    def _():
        pl.semaphore_wait(barrier, 2 + NY - 1 + NROW - 1 + len(FAR))
        for d in range(1, NY):
            piece_y_copy(d).start()
        edge_f[0, z] = f_cut[y, 15, 0]

    @pl.when(row < second_root)
    def _():
        pl.semaphore_wait(barrier, 2 + NY - 1 + 2)

    for c in range(CHUNKS):
        for d in range(1, NY):
            y_copy(c, d).start()
        if c < 2:
            for way in range(2):
                own_copy(c, way).start()

    def hop_copy(unit, hop, way):
        c, s = unit
        n = c * 2 + s
        block = (z - (hop - 1) + NZ) % NZ if way == 0 else (z + hop - 1) % NZ
        if hop == 1:
            ref = buf.at[span(c), s, pl.ds(1, NY - 1), block]
        elif hop < 4:
            ref = buf.at[span(c), s, :, block]
        else:
            ref = buf.at[span(c), s, pl.ds(2 * way, 2), block]
        return remote(
            ref, ref, zsend.at[way, n, hop - 1], zrecv.at[way, n, hop - 1],
            at(row, y, up if way == 0 else down),
        )

    def edge_copy(d):
        to = (y + d) % NY
        return remote(edge_out.at[to], edge_in.at[y], esend.at[d - 1], erecv.at[d - 1], at(row, to, z))

    def back_copy(c, d):
        to = (y + d) % NY
        return remote(
            back_out.at[to, span(c)], back_in.at[y, span(c)], bsend.at[c, d - 1], brecv.at[c, d - 1], at(row, to, z)
        )

    def wait_last(unit):
        for way in range(2):
            hop_copy(unit, 4, way).wait_recv()

    def subtract(j, q, change):
        rows = pl.ds(4 * j + q, 64, stride=64)
        upd_ref[rows, :] = x_v[rows, :] - change.astype(F32)

    own_seen, y_seen = set(), set()
    multiplied = stored = False
    own.wait()
    for step in ORDER:
        if step[0] in UNITS and len(step) == 2:
            n = UNITS.index(step[0])
            unit, hop = (n // 2, n % 2), int(step[1])
            c = unit[0]
            if hop == 1 and c not in y_seen:
                y_seen.add(c)
                for d in range(1, NY):
                    y_copy(c, d).wait_recv()
            if hop == 2 and min(c, 1) not in own_seen:
                own_seen.add(min(c, 1))
                for way in range(2):
                    own_copy(min(c, 1), way).wait_recv()
            for way in range(2):
                if hop > 1:
                    hop_copy(unit, hop - 1, way).wait_recv()
                hop_copy(unit, hop, way).start()
        elif step == "e0":

            @pl.when(row >= second_root)
            def _():
                share_narrow(0, first_root)

        elif step == "e1":

            @pl.when(row == second_root)
            def _():
                for d in range(1, NY):
                    piece_y_copy(d).wait_recv()
                for d in range(1, NZ):
                    piece_z_copy(d).start()

        elif step == "n0":

            @pl.when(row < second_root)
            def _():
                share_narrow(0, first_root)

        elif step == "edge":

            @pl.when(row == second_root)
            def _():
                take_narrow(0)
                for d in range(1, NZ):
                    piece_z_copy(d).wait_recv()
                product = jnp.dot(
                    lhs[:, :512], edge_f[...].reshape(512, 128), preferred_element_type=F32
                )
                edge_out[...] = product.reshape(NY, 64, 128)
                for d in range(1, NY):
                    edge_copy(d).start()
                edge_in[y] = edge_out[y]

        elif step == "solve":

            @pl.when(row == second_root)
            def _():
                for d in range(1, NY):
                    edge_copy(d).wait_recv()
                change = jnp.concatenate([edge_in[q] for q in range(NY)], axis=1)
                nar[1, y], low[1] = halves(times_inverse(block_of_rhs(15) - change))
                spread_row(1, second_root)

        elif step == "share":
            share_narrow(1, second_root)
        elif step[0] == "c":
            c = int(step[1])
            if not multiplied:
                multiplied = True

                @pl.when(row != second_root)
                def _():
                    take_narrow(0)

                take_narrow(1)
            for s in range(2):
                wait_last((c, s))
            for j in range(BOUNDS[c], BOUNDS[c + 1], 2):
                width = min(2, BOUNDS[c + 1] - j)
                factor = jnp.concatenate([buf[j + i].reshape(1024, 128) for i in range(width)], axis=1)
                change = jnp.dot(lhs[...], factor, preferred_element_type=F32).astype(BF16)
                for i in range(width):
                    back_out[:, j + i] = change[:, i * 128:(i + 1) * 128].reshape(NY, 64, 128)
            for d in range(1, NY):
                back_copy(c, d).start()
        else:
            c = int(step[1])
            if not stored:
                stored = True
                for s in range(2):
                    store_solved(s, NROW - 1 - s)
            for d in range(1, NY):
                back_copy(c, d).wait_recv()
            back_in[y, span(c)] = back_out[y, span(c)]
            for q in range(NY):
                for j in range(BOUNDS[c], BOUNDS[c + 1]):
                    if j < 15:
                        subtract(j, q, back_in[q, j])
                    else:
                        @pl.when(row < second_root)
                        def _(q=q):
                            subtract(15, q, back_in[q, 15])

                        @pl.when(row == second_root)
                        def _(q=q):
                            subtract(15, q, edge_in[q])

                        @pl.when(row == first_root)
                        def _(q=q):
                            subtract(15, q, jnp.zeros((64, 128), F32))

    for c in range(CHUNKS):
        for d in range(1, NY):
            y_copy(c, d).wait_send()
            back_copy(c, d).wait_send()
        for s in range(2):
            for hop in range(1, 5):
                for way in range(2):
                    hop_copy((c, s), hop, way).wait_send()
    for part in range(2):
        for way in range(2):
            own_copy(part, way).wait_send()
    for s in range(2):
        for d in range(1, NY):
            narrow_copy(s, d).wait_send()
    for s in range(2):
        root = NROW - 1 - s

        @pl.when(row == root)
        def _():
            for part in range(2):
                for t in range(NROW):
                    if t != root:
                        row_copy(s, part, t).wait_send()

    @pl.when(row == second_root)
    def _():
        for d in range(1, NY):
            piece_y_copy(d).wait_send()
            edge_copy(d).wait_send()
        for d in range(1, NZ):
            piece_z_copy(d).wait_send()


def on_device(rhs, factor_rows, diag_inverse):
    dma = pltpu.SemaphoreType.DMA
    any_space = pl.BlockSpec(memory_space=pl.ANY)
    in_hbm = functools.partial(pltpu.with_memory_space_constraint, memory_space=pltpu.HBM)
    solved, updated = pl.pallas_call(
        kernel,
        out_shape=(
            pltpu.VMEM((2, 64, 512), F32),
            pltpu.VMEM((4096, 128), F32),
        ),
        in_specs=[any_space] * 3,
        out_specs=[pl.BlockSpec(memory_space=pltpu.VMEM)] * 2,
        scratch_shapes=[
            pltpu.VMEM((4096, 128), F32),
            pltpu.VMEM((512, 512), BF16),
            pltpu.VMEM((4, 512, 128), F32),
            pltpu.VMEM((NY, 16, 2, 16, 128), BF16),
            pltpu.VMEM((512, 512), F32),
            pltpu.VMEM((2, 512, 512), BF16),
            pltpu.VMEM((16, 2, NY, NZ, 16, 128), BF16),
            pltpu.VMEM((NY, NZ, 16, 128), BF16),
            pltpu.VMEM((2, NY, 64, 512), BF16),
            pltpu.VMEM((256, 1024), BF16),
            pltpu.VMEM((2, 64, 512), BF16),
            pltpu.VMEM((NY, 64, 128), F32),
            pltpu.VMEM((NY, 64, 128), F32),
            pltpu.VMEM((NY, 16, 64, 128), BF16),
            pltpu.VMEM((NY, 16, 64, 128), BF16),
            dma((3,)),
            dma,
            dma((CHUNKS, NY - 1)),
            dma((CHUNKS, NY - 1)),
            dma((2, 2)),
            dma((2, 2)),
            dma((2, CHUNKS * 2, 4)),
            dma((2, CHUNKS * 2, 4)),
            dma((2, 2, NROW)),
            dma((2, 2)),
            dma((2, NY - 1)),
            dma((2, NY - 1)),
            dma((NY - 1,)),
            dma((NY - 1,)),
            dma((NY - 1,)),
            dma((NY - 1,)),
            dma((NZ - 1,)),
            dma((NZ - 1,)),
            dma((CHUNKS, NY - 1)),
            dma((CHUNKS, NY - 1)),
        ],
        compiler_params=pltpu.CompilerParams(
            collective_id=0, has_side_effects=True, vmem_limit_bytes=48 * 1024 * 1024
        ),
        name="back_substitution",
    )(
        in_hbm(rhs.reshape(4096, 128)),
        in_hbm(factor_rows.reshape(512, 512)),
        in_hbm(diag_inverse),
    )
    return solved, updated.reshape(rhs.shape)


def solution(mesh):
    return jax.shard_map(
        on_device,
        mesh=mesh,
        in_specs=(P("col", None, "row", None), P(None, "col", None, "row", None), P()),
        out_specs=(P(None, "col", None), P("col", None, "row", None)),
        check_vma=False,
    )
```

```python
import functools

import jax
import jax.numpy as jnp
from jax import lax
from jax.experimental import pallas as pl
from jax.experimental.pallas import tpu as pltpu
from jax.sharding import PartitionSpec as P

NY, NZ, NROW = 4, 8, 8
CHUNKS = 4
UNITS = "ABCDEFGH"
ROW_TARGETS = (6, 2, 3, 0, 1, 4, 5, 7)
FAR = (2, 3, 4, 5, 6)
BF16, F32 = jnp.bfloat16, jnp.float32
BOUNDS = (0, 5, 9, 13, 16)
ORDER = (
    "e1", "A1", "B1", "e0", "E1", "D1", "A2", "G1", "H1", "B2", "C1",
    "n0", "A3", "D2", "edge", "C2", "A4", "E2", "solve", "B3", "F1", "C3",
    "D3", "share", "B4", "G2", "F2", "D4", "H2", "C4", "E3", "c0", "F3",
    "H3", "G3", "c1", "E4", "F4", "H4", "G4", "c2", "c3", "f0", "f1",
    "f2", "f3",
)


def kernel(
    x_hbm, f_hbm, d_hbm, sol_ref, upd_ref,
    x_v, f_v, f_wide, f_cut, d_v, d_cut, buf, edge_f, nar, lhs, low, edge_out, edge_in, back_out, back_in,
    in_sem, own_sem, ysend, yrecv, osend, orecv, zsend, zrecv, rsend, rrecv, nsend, nrecv,
    esend, erecv, pysend, pyrecv, pzsend, pzrecv, bsend, brecv,
):
    row = lax.axis_index("row")
    col = lax.axis_index("col")
    y = col // NZ
    z = col % NZ
    up, down = (z + 1) % NZ, (z + NZ - 1) % NZ
    first_root, second_root = NROW - 1, NROW - 2

    def at(row_, y_, z_):
        return (row_, y_ * NZ + z_)

    def remote(src, dst, send, recv, device):
        return pltpu.make_async_remote_copy(
            src_ref=src, dst_ref=dst, send_sem=send, recv_sem=recv,
            device_id=device, device_id_type=pl.DeviceIdType.MESH,
        )

    f_in = pltpu.make_async_copy(f_hbm, f_v, in_sem.at[0])
    x_in = pltpu.make_async_copy(x_hbm, x_v, in_sem.at[1])
    d_in = pltpu.make_async_copy(d_hbm.at[jnp.where(row == first_root, 0, 1)], d_v, in_sem.at[2])
    f_in.start()
    d_in.start()
    x_in.start()

    def signal(device):
        pl.semaphore_signal(barrier, inc=1, device_id=device, device_id_type=pl.DeviceIdType.MESH)

    barrier = pltpu.get_barrier_semaphore()
    signal(at(row, y, up))
    signal(at(row, y, down))
    for d in range(1, NY):
        signal(at(row, (y + d) % NY, z))
    for root in (first_root, second_root):
        for t in range(NROW):
            if t != root:
                if t < second_root:
                    @pl.when(row == root)
                    def _(t=t):
                        signal(at(t, y, z))

                    @pl.when(row == t)
                    def _(root=root):
                        signal(at(root, y, z))
                else:
                    @pl.when(row == root)
                    def _(t=t):
                        signal(at(t, y, z))

    @pl.when(row == second_root)
    def _():
        for d in FAR:
            signal(at(row, y, (z + d) % NZ))

    f_in.wait()
    for l in range(4):
        f_wide[l] = f_v[:, l * 128:(l + 1) * 128].astype(F32)
    for q in range(NY):
        for j in range(16):
            f_cut[q, j] = f_wide[q, pl.ds(j, 32, stride=16), :].astype(BF16).reshape(2, 16, 128)
    own = pltpu.make_async_copy(f_cut.at[y], buf.at[:, :, 0, z], own_sem)
    own.start()

    def span(c):
        return pl.ds(BOUNDS[c], BOUNDS[c + 1] - BOUNDS[c])

    def y_copy(c, d):
        to = (y + d) % NY
        return remote(
            f_cut.at[to, span(c)], buf.at[span(c), :, NY - d, z],
            ysend.at[c, d - 1], yrecv.at[c, d - 1], at(row, to, z),
        )

    def own_copy(part, way):
        blocks = span(0) if part == 0 else pl.ds(BOUNDS[1], 16 - BOUNDS[1])
        return remote(
            f_cut.at[y, blocks], buf.at[blocks, :, 0, z], osend.at[part, way], orecv.at[part, way],
            at(row, y, up if way == 0 else down),
        )

    def piece_y_copy(d):
        to = (y + d) % NY
        return remote(
            f_cut.at[to, 15, 0], edge_f.at[NY - d, z], pysend.at[d - 1], pyrecv.at[d - 1], at(row, to, z)
        )

    def piece_z_copy(d):
        return remote(
            edge_f.at[:, z], edge_f.at[:, z], pzsend.at[d - 1], pzrecv.at[d - 1], at(row, y, (z + d) % NZ)
        )

    def block_of_rhs(j):
        return jnp.concatenate(
            [x_v[pl.ds(4 * j + l, 64, stride=64), :] for l in range(4)], axis=1
        )

    def halves(value):
        high = value.astype(BF16)
        return high, (value - high.astype(F32)).astype(BF16)

    def times_inverse(value):
        high, rest = halves(value)
        dot = functools.partial(jnp.dot, preferred_element_type=F32)
        return dot(high, d_cut[0]) + (dot(high, d_cut[1]) + dot(rest, d_cut[0]))

    def spread_row(s, root):
        for part in range(2):
            for t in ROW_TARGETS:
                if t != root:
                    row_copy(s, part, t).start()

    def row_copy(s, part, t):
        ref = nar.at[s, y] if part == 0 else low.at[s]
        return remote(ref, ref, rsend.at[s, part, t], rrecv.at[s, part], at(t, y, z))

    def narrow_copy(s, d):
        ref = nar.at[s, y]
        return remote(ref, ref, nsend.at[s, d - 1], nrecv.at[s, d - 1], at(row, (y + d) % NY, z))

    def share_narrow(s, root):
        @pl.when(row != root)
        def _():
            row_copy(s, 0, 0).wait_recv()

        for d in range(1, NY):
            narrow_copy(s, d).start()

    def take_narrow(s):
        for d in range(1, NY):
            narrow_copy(s, d).wait_recv()
        for d in range(NY):
            columns = pl.ds(pl.multiple_of((y + d) % NY * 128, 128), 128)
            for q in range(NY):
                lhs[q * 64:(q + 1) * 64, s * 512 + d * 128:s * 512 + (d + 1) * 128] = nar[s, q, :, columns]

    def store_solved(s, root):
        @pl.when(row != root)
        def _():
            row_copy(s, 1, 0).wait_recv()

        sol_ref[s] = nar[s, y].astype(F32) + low[s].astype(F32)

    @pl.when(row == first_root)
    def _():
        pl.semaphore_wait(barrier, 2 + NY - 1 + NROW - 1)

    @pl.when(row == second_root)
    def _():
        pl.semaphore_wait(barrier, 2 + NY - 1 + NROW - 1 + len(FAR))
        for d in range(1, NY):
            piece_y_copy(d).start()
        edge_f[0, z] = f_cut[y, 15, 0]

    @pl.when(row < second_root)
    def _():
        pl.semaphore_wait(barrier, 2 + NY - 1 + 2)

    for c in range(CHUNKS):
        for d in range(1, NY):
            y_copy(c, d).start()
        if c < 2:
            for way in range(2):
                own_copy(c, way).start()

    d_in.wait()
    x_in.wait()

    @pl.when(row >= second_root)
    def _():
        for i in range(4):
            rows = slice(i * 128, (i + 1) * 128)
            d_cut[0, rows], d_cut[1, rows] = halves(d_v[rows])

    @pl.when(row == first_root)
    def _():
        nar[0, y], low[0] = halves(times_inverse(block_of_rhs(15)))
        spread_row(0, first_root)

    def hop_copy(unit, hop, way):
        c, s = unit
        n = c * 2 + s
        block = (z - (hop - 1) + NZ) % NZ if way == 0 else (z + hop - 1) % NZ
        if hop == 1:
            ref = buf.at[span(c), s, pl.ds(1, NY - 1), block]
        elif hop < 4:
            ref = buf.at[span(c), s, :, block]
        else:
            ref = buf.at[span(c), s, pl.ds(2 * way, 2), block]
        return remote(
            ref, ref, zsend.at[way, n, hop - 1], zrecv.at[way, n, hop - 1],
            at(row, y, up if way == 0 else down),
        )

    def edge_copy(d):
        to = (y + d) % NY
        return remote(edge_out.at[to], edge_in.at[y], esend.at[d - 1], erecv.at[d - 1], at(row, to, z))

    def back_copy(c, d):
        to = (y + d) % NY
        return remote(
            back_out.at[to, span(c)], back_in.at[y, span(c)], bsend.at[c, d - 1], brecv.at[c, d - 1], at(row, to, z)
        )

    def wait_last(unit):
        for way in range(2):
            hop_copy(unit, 4, way).wait_recv()

    def subtract(j, q, change):
        rows = pl.ds(4 * j + q, 64, stride=64)
        upd_ref[rows, :] = x_v[rows, :] - change.astype(F32)

    own_seen, y_seen = set(), set()
    multiplied = stored = False
    own.wait()
    for step in ORDER:
        if step[0] in UNITS and len(step) == 2:
            n = UNITS.index(step[0])
            unit, hop = (n // 2, n % 2), int(step[1])
            c = unit[0]
            if hop == 1 and c not in y_seen:
                y_seen.add(c)
                for d in range(1, NY):
                    y_copy(c, d).wait_recv()
            if hop == 2 and min(c, 1) not in own_seen:
                own_seen.add(min(c, 1))
                for way in range(2):
                    own_copy(min(c, 1), way).wait_recv()
            for way in range(2):
                if hop > 1:
                    hop_copy(unit, hop - 1, way).wait_recv()
                hop_copy(unit, hop, way).start()
        elif step == "e0":

            @pl.when(row >= second_root)
            def _():
                share_narrow(0, first_root)

        elif step == "e1":

            @pl.when(row == second_root)
            def _():
                for d in range(1, NY):
                    piece_y_copy(d).wait_recv()
                for d in range(1, NZ):
                    piece_z_copy(d).start()

        elif step == "n0":

            @pl.when(row < second_root)
            def _():
                share_narrow(0, first_root)

        elif step == "edge":

            @pl.when(row == second_root)
            def _():
                take_narrow(0)
                for d in range(1, NZ):
                    piece_z_copy(d).wait_recv()
                product = jnp.dot(
                    lhs[:, :512], edge_f[...].reshape(512, 128), preferred_element_type=F32
                )
                edge_out[...] = product.reshape(NY, 64, 128)
                for d in range(1, NY):
                    edge_copy(d).start()
                edge_in[y] = edge_out[y]

        elif step == "solve":

            @pl.when(row == second_root)
            def _():
                for d in range(1, NY):
                    edge_copy(d).wait_recv()
                change = jnp.concatenate([edge_in[q] for q in range(NY)], axis=1)
                nar[1, y], low[1] = halves(times_inverse(block_of_rhs(15) - change))
                spread_row(1, second_root)

        elif step == "share":
            share_narrow(1, second_root)
        elif step[0] == "c":
            c = int(step[1])
            if not multiplied:
                multiplied = True

                @pl.when(row != second_root)
                def _():
                    take_narrow(0)

                take_narrow(1)
            for s in range(2):
                wait_last((c, s))
            for j in range(BOUNDS[c], BOUNDS[c + 1], 2):
                width = min(2, BOUNDS[c + 1] - j)
                factor = jnp.concatenate([buf[j + i].reshape(1024, 128) for i in range(width)], axis=1)
                change = jnp.dot(lhs[...], factor, preferred_element_type=F32).astype(BF16)
                for i in range(width):
                    back_out[:, j + i] = change[:, i * 128:(i + 1) * 128].reshape(NY, 64, 128)
            for d in range(1, NY):
                back_copy(c, d).start()
        else:
            c = int(step[1])
            if not stored:
                stored = True
                for s in range(2):
                    store_solved(s, NROW - 1 - s)
            for d in range(1, NY):
                back_copy(c, d).wait_recv()
            back_in[y, span(c)] = back_out[y, span(c)]
            for q in range(NY):
                for j in range(BOUNDS[c], BOUNDS[c + 1]):
                    if j < 15:
                        subtract(j, q, back_in[q, j])
                    else:
                        @pl.when(row < second_root)
                        def _(q=q):
                            subtract(15, q, back_in[q, 15])

                        @pl.when(row == second_root)
                        def _(q=q):
                            subtract(15, q, edge_in[q])

                        @pl.when(row == first_root)
                        def _(q=q):
                            subtract(15, q, jnp.zeros((64, 128), F32))

    for c in range(CHUNKS):
        for d in range(1, NY):
            y_copy(c, d).wait_send()
            back_copy(c, d).wait_send()
        for s in range(2):
            for hop in range(1, 5):
                for way in range(2):
                    hop_copy((c, s), hop, way).wait_send()
    for part in range(2):
        for way in range(2):
            own_copy(part, way).wait_send()
    for s in range(2):
        for d in range(1, NY):
            narrow_copy(s, d).wait_send()
    for s in range(2):
        root = NROW - 1 - s

        @pl.when(row == root)
        def _():
            for part in range(2):
                for t in range(NROW):
                    if t != root:
                        row_copy(s, part, t).wait_send()

    @pl.when(row == second_root)
    def _():
        for d in range(1, NY):
            piece_y_copy(d).wait_send()
            edge_copy(d).wait_send()
        for d in range(1, NZ):
            piece_z_copy(d).wait_send()


def on_device(rhs, factor_rows, diag_inverse):
    dma = pltpu.SemaphoreType.DMA
    any_space = pl.BlockSpec(memory_space=pl.ANY)
    in_hbm = functools.partial(pltpu.with_memory_space_constraint, memory_space=pltpu.HBM)
    solved, updated = pl.pallas_call(
        kernel,
        out_shape=(
            pltpu.VMEM((2, 64, 512), F32),
            pltpu.VMEM((4096, 128), F32),
        ),
        in_specs=[any_space] * 3,
        out_specs=[pl.BlockSpec(memory_space=pltpu.VMEM)] * 2,
        scratch_shapes=[
            pltpu.VMEM((4096, 128), F32),
            pltpu.VMEM((512, 512), BF16),
            pltpu.VMEM((4, 512, 128), F32),
            pltpu.VMEM((NY, 16, 2, 16, 128), BF16),
            pltpu.VMEM((512, 512), F32),
            pltpu.VMEM((2, 512, 512), BF16),
            pltpu.VMEM((16, 2, NY, NZ, 16, 128), BF16),
            pltpu.VMEM((NY, NZ, 16, 128), BF16),
            pltpu.VMEM((2, NY, 64, 512), BF16),
            pltpu.VMEM((256, 1024), BF16),
            pltpu.VMEM((2, 64, 512), BF16),
            pltpu.VMEM((NY, 64, 128), F32),
            pltpu.VMEM((NY, 64, 128), F32),
            pltpu.VMEM((NY, 16, 64, 128), BF16),
            pltpu.VMEM((NY, 16, 64, 128), BF16),
            dma((3,)),
            dma,
            dma((CHUNKS, NY - 1)),
            dma((CHUNKS, NY - 1)),
            dma((2, 2)),
            dma((2, 2)),
            dma((2, CHUNKS * 2, 4)),
            dma((2, CHUNKS * 2, 4)),
            dma((2, 2, NROW)),
            dma((2, 2)),
            dma((2, NY - 1)),
            dma((2, NY - 1)),
            dma((NY - 1,)),
            dma((NY - 1,)),
            dma((NY - 1,)),
            dma((NY - 1,)),
            dma((NZ - 1,)),
            dma((NZ - 1,)),
            dma((CHUNKS, NY - 1)),
            dma((CHUNKS, NY - 1)),
        ],
        compiler_params=pltpu.CompilerParams(
            collective_id=0, has_side_effects=True, vmem_limit_bytes=48 * 1024 * 1024
        ),
        name="back_substitution",
    )(
        in_hbm(rhs.reshape(4096, 128)),
        in_hbm(factor_rows.reshape(512, 512)),
        in_hbm(diag_inverse),
    )
    return solved, updated.reshape(rhs.shape)


def solution(mesh):
    return jax.shard_map(
        on_device,
        mesh=mesh,
        in_specs=(P("col", None, "row", None), P(None, "col", None, "row", None), P()),
        out_specs=(P(None, "col", None), P("col", None, "row", None)),
        check_vma=False,
    )
```

```python
import functools

import jax
import jax.numpy as jnp
from jax import lax
from jax.experimental import pallas as pl
from jax.experimental.pallas import tpu as pltpu
from jax.sharding import PartitionSpec as P

NY, NZ, NROW = 4, 8, 8
CHUNKS = 4
UNITS = "ABCDEFGH"
ROW_TARGETS = (6, 2, 3, 0, 1, 4, 5, 7)
FAR = (2, 3, 4, 5, 6)
FARTHEST_FIRST = (2, 1, 3)
BF16, F32 = jnp.bfloat16, jnp.float32
BOUNDS = (0, 5, 9, 13, 16)
ORDER = (
    "e1", "A1", "B1", "e0", "E1", "D1", "A2", "G1", "H1", "B2", "C1",
    "n0", "A3", "D2", "edge", "C2", "A4", "E2", "solve", "B3", "F1", "C3",
    "D3", "share", "B4", "G2", "F2", "D4", "H2", "C4", "E3", "c0", "F3",
    "H3", "G3", "c1", "E4", "F4", "H4", "G4", "c2", "c3", "f0", "f1",
    "f2", "f3",
)


def kernel(
    x_hbm, f_hbm, d_hbm, sol_ref, upd_ref,
    x_v, f_v, f_wide, f_cut, d_v, d_cut, buf, edge_f, nar, lhs, low, edge_out, edge_in, back_out, back_in,
    in_sem, own_sem, ysend, yrecv, osend, orecv, zsend, zrecv, rsend, rrecv, nsend, nrecv,
    esend, erecv, pysend, pyrecv, pzsend, pzrecv, bsend, brecv,
):
    row = lax.axis_index("row")
    col = lax.axis_index("col")
    y = col // NZ
    z = col % NZ
    up, down = (z + 1) % NZ, (z + NZ - 1) % NZ
    first_root, second_root = NROW - 1, NROW - 2

    def at(row_, y_, z_):
        return (row_, y_ * NZ + z_)

    def remote(src, dst, send, recv, device):
        return pltpu.make_async_remote_copy(
            src_ref=src, dst_ref=dst, send_sem=send, recv_sem=recv,
            device_id=device, device_id_type=pl.DeviceIdType.MESH,
        )

    f_in = pltpu.make_async_copy(f_hbm, f_v, in_sem.at[0])
    x_in = pltpu.make_async_copy(x_hbm, x_v, in_sem.at[1])
    d_in = pltpu.make_async_copy(d_hbm.at[jnp.where(row == first_root, 0, 1)], d_v, in_sem.at[2])
    f_in.start()
    d_in.start()
    x_in.start()

    def signal(device):
        pl.semaphore_signal(barrier, inc=1, device_id=device, device_id_type=pl.DeviceIdType.MESH)

    barrier = pltpu.get_barrier_semaphore()
    signal(at(row, y, up))
    signal(at(row, y, down))
    for d in range(1, NY):
        signal(at(row, (y + d) % NY, z))
    for root in (first_root, second_root):
        for t in range(NROW):
            if t != root:
                if t < second_root:
                    @pl.when(row == root)
                    def _(t=t):
                        signal(at(t, y, z))

                    @pl.when(row == t)
                    def _(root=root):
                        signal(at(root, y, z))
                else:
                    @pl.when(row == root)
                    def _(t=t):
                        signal(at(t, y, z))

    @pl.when(row == second_root)
    def _():
        for d in FAR:
            signal(at(row, y, (z + d) % NZ))

    f_in.wait()
    for l in range(4):
        f_wide[l] = f_v[:, l * 128:(l + 1) * 128].astype(F32)
    for q in range(NY):
        for j in range(16):
            f_cut[q, j] = f_wide[q, pl.ds(j, 32, stride=16), :].astype(BF16).reshape(2, 16, 128)
    own = pltpu.make_async_copy(f_cut.at[y], buf.at[:, :, 0, z], own_sem)
    own.start()

    def span(c):
        return pl.ds(BOUNDS[c], BOUNDS[c + 1] - BOUNDS[c])

    def y_copy(c, d):
        to = (y + d) % NY
        return remote(
            f_cut.at[to, span(c)], buf.at[span(c), :, NY - d, z],
            ysend.at[c, d - 1], yrecv.at[c, d - 1], at(row, to, z),
        )

    def own_copy(part, way):
        blocks = span(0) if part == 0 else pl.ds(BOUNDS[1], 16 - BOUNDS[1])
        return remote(
            f_cut.at[y, blocks], buf.at[blocks, :, 0, z], osend.at[part, way], orecv.at[part, way],
            at(row, y, up if way == 0 else down),
        )

    def piece_y_copy(d):
        to = (y + d) % NY
        return remote(
            f_cut.at[to, 15, 0], edge_f.at[NY - d, z], pysend.at[d - 1], pyrecv.at[d - 1], at(row, to, z)
        )

    def piece_z_copy(d):
        return remote(
            edge_f.at[:, z], edge_f.at[:, z], pzsend.at[d - 1], pzrecv.at[d - 1], at(row, y, (z + d) % NZ)
        )

    def block_of_rhs(j):
        return jnp.concatenate(
            [x_v[pl.ds(4 * j + l, 64, stride=64), :] for l in range(4)], axis=1
        )

    def halves(value):
        high = value.astype(BF16)
        return high, (value - high.astype(F32)).astype(BF16)

    def times_inverse(value):
        high, rest = halves(value)
        dot = functools.partial(jnp.dot, preferred_element_type=F32)
        return dot(high, d_cut[0]) + (dot(high, d_cut[1]) + dot(rest, d_cut[0]))

    def spread_row(s, root):
        for part in range(2):
            for t in ROW_TARGETS:
                if t != root:
                    row_copy(s, part, t).start()

    def row_copy(s, part, t):
        ref = nar.at[s, y] if part == 0 else low.at[s]
        return remote(ref, ref, rsend.at[s, part, t], rrecv.at[s, part], at(t, y, z))

    def narrow_copy(s, d):
        ref = nar.at[s, y]
        return remote(ref, ref, nsend.at[s, d - 1], nrecv.at[s, d - 1], at(row, (y + d) % NY, z))

    def share_narrow(s, root):
        @pl.when(row != root)
        def _():
            row_copy(s, 0, 0).wait_recv()

        for d in range(1, NY):
            narrow_copy(s, d).start()

    def take_narrow(s):
        for d in range(1, NY):
            narrow_copy(s, d).wait_recv()
        for d in range(NY):
            columns = pl.ds(pl.multiple_of((y + d) % NY * 128, 128), 128)
            for q in range(NY):
                lhs[q * 64:(q + 1) * 64, s * 512 + d * 128:s * 512 + (d + 1) * 128] = nar[s, q, :, columns]

    def store_solved(s, root):
        @pl.when(row != root)
        def _():
            row_copy(s, 1, 0).wait_recv()

        sol_ref[s] = nar[s, y].astype(F32) + low[s].astype(F32)

    @pl.when(row == first_root)
    def _():
        pl.semaphore_wait(barrier, 2 + NY - 1 + NROW - 1)

    @pl.when(row == second_root)
    def _():
        pl.semaphore_wait(barrier, 2 + NY - 1 + NROW - 1 + len(FAR))
        for d in range(1, NY):
            piece_y_copy(d).start()
        edge_f[0, z] = f_cut[y, 15, 0]

    @pl.when(row < second_root)
    def _():
        pl.semaphore_wait(barrier, 2 + NY - 1 + 2)

    for c in range(CHUNKS):
        for d in range(1, NY):
            y_copy(c, d).start()
        if c < 2:
            for way in range(2):
                own_copy(c, way).start()

    d_in.wait()
    x_in.wait()

    @pl.when(row >= second_root)
    def _():
        for i in range(4):
            rows = slice(i * 128, (i + 1) * 128)
            d_cut[0, rows], d_cut[1, rows] = halves(d_v[rows])

    @pl.when(row == first_root)
    def _():
        nar[0, y], low[0] = halves(times_inverse(block_of_rhs(15)))
        spread_row(0, first_root)

    def hop_copy(unit, hop, way):
        c, s = unit
        n = c * 2 + s
        block = (z - (hop - 1) + NZ) % NZ if way == 0 else (z + hop - 1) % NZ
        if hop == 1:
            ref = buf.at[span(c), s, pl.ds(1, NY - 1), block]
        elif hop < 4:
            ref = buf.at[span(c), s, :, block]
        else:
            ref = buf.at[span(c), s, pl.ds(2 * way, 2), block]
        return remote(
            ref, ref, zsend.at[way, n, hop - 1], zrecv.at[way, n, hop - 1],
            at(row, y, up if way == 0 else down),
        )

    def edge_copy(d):
        to = (y + d) % NY
        return remote(edge_out.at[to], edge_in.at[y], esend.at[d - 1], erecv.at[d - 1], at(row, to, z))

    def back_copy(c, d):
        to = (y + d) % NY
        return remote(
            back_out.at[to, span(c)], back_in.at[y, span(c)], bsend.at[c, d - 1], brecv.at[c, d - 1], at(row, to, z)
        )

    def wait_last(unit):
        for way in range(2):
            hop_copy(unit, 4, way).wait_recv()

    def subtract(j, q, change):
        rows = pl.ds(4 * j + q, 64, stride=64)
        upd_ref[rows, :] = x_v[rows, :] - change.astype(F32)

    own_seen, y_seen = set(), set()
    multiplied = stored = False
    own.wait()
    for step in ORDER:
        if step[0] in UNITS and len(step) == 2:
            n = UNITS.index(step[0])
            unit, hop = (n // 2, n % 2), int(step[1])
            c = unit[0]
            if hop == 1 and c not in y_seen:
                y_seen.add(c)
                for d in range(1, NY):
                    y_copy(c, d).wait_recv()
            if hop == 2 and min(c, 1) not in own_seen:
                own_seen.add(min(c, 1))
                for way in range(2):
                    own_copy(min(c, 1), way).wait_recv()
            for way in range(2):
                if hop > 1:
                    hop_copy(unit, hop - 1, way).wait_recv()
                hop_copy(unit, hop, way).start()
        elif step == "e0":

            @pl.when(row >= second_root)
            def _():
                share_narrow(0, first_root)

        elif step == "e1":

            @pl.when(row == second_root)
            def _():
                for d in range(1, NY):
                    piece_y_copy(d).wait_recv()
                for d in range(1, NZ):
                    piece_z_copy(d).start()

        elif step == "n0":

            @pl.when(row < second_root)
            def _():
                share_narrow(0, first_root)

        elif step == "edge":

            @pl.when(row == second_root)
            def _():
                take_narrow(0)
                for d in range(1, NZ):
                    piece_z_copy(d).wait_recv()
                product = jnp.dot(
                    lhs[:, :512], edge_f[...].reshape(512, 128), preferred_element_type=F32
                )
                edge_out[...] = product.reshape(NY, 64, 128)
                for d in range(1, NY):
                    edge_copy(d).start()
                edge_in[y] = edge_out[y]

        elif step == "solve":

            @pl.when(row == second_root)
            def _():
                for d in range(1, NY):
                    edge_copy(d).wait_recv()
                change = jnp.concatenate([edge_in[q] for q in range(NY)], axis=1)
                nar[1, y], low[1] = halves(times_inverse(block_of_rhs(15) - change))
                spread_row(1, second_root)

        elif step == "share":
            share_narrow(1, second_root)
        elif step[0] == "c":
            c = int(step[1])
            if not multiplied:
                multiplied = True

                @pl.when(row != second_root)
                def _():
                    take_narrow(0)

                take_narrow(1)
            for s in range(2):
                wait_last((c, s))
            for j in range(BOUNDS[c], BOUNDS[c + 1], 2):
                width = min(2, BOUNDS[c + 1] - j)
                factor = jnp.concatenate([buf[j + i].reshape(1024, 128) for i in range(width)], axis=1)
                change = jnp.dot(lhs[...], factor, preferred_element_type=F32).astype(BF16)
                for i in range(width):
                    back_out[:, j + i] = change[:, i * 128:(i + 1) * 128].reshape(NY, 64, 128)
            for d in FARTHEST_FIRST:
                back_copy(c, d).start()
        else:
            c = int(step[1])
            if not stored:
                stored = True
                for s in range(2):
                    store_solved(s, NROW - 1 - s)
            for d in range(1, NY):
                back_copy(c, d).wait_recv()
            back_in[y, span(c)] = back_out[y, span(c)]
            for q in range(NY):
                for j in range(BOUNDS[c], BOUNDS[c + 1]):
                    if j < 15:
                        subtract(j, q, back_in[q, j])
                    else:
                        @pl.when(row < second_root)
                        def _(q=q):
                            subtract(15, q, back_in[q, 15])

                        @pl.when(row == second_root)
                        def _(q=q):
                            subtract(15, q, edge_in[q])

                        @pl.when(row == first_root)
                        def _(q=q):
                            subtract(15, q, jnp.zeros((64, 128), F32))

    for c in range(CHUNKS):
        for d in range(1, NY):
            y_copy(c, d).wait_send()
            back_copy(c, d).wait_send()
        for s in range(2):
            for hop in range(1, 5):
                for way in range(2):
                    hop_copy((c, s), hop, way).wait_send()
    for part in range(2):
        for way in range(2):
            own_copy(part, way).wait_send()
    for s in range(2):
        for d in range(1, NY):
            narrow_copy(s, d).wait_send()
    for s in range(2):
        root = NROW - 1 - s

        @pl.when(row == root)
        def _():
            for part in range(2):
                for t in range(NROW):
                    if t != root:
                        row_copy(s, part, t).wait_send()

    @pl.when(row == second_root)
    def _():
        for d in range(1, NY):
            piece_y_copy(d).wait_send()
            edge_copy(d).wait_send()
        for d in range(1, NZ):
            piece_z_copy(d).wait_send()


def on_device(rhs, factor_rows, diag_inverse):
    dma = pltpu.SemaphoreType.DMA
    any_space = pl.BlockSpec(memory_space=pl.ANY)
    in_hbm = functools.partial(pltpu.with_memory_space_constraint, memory_space=pltpu.HBM)
    solved, updated = pl.pallas_call(
        kernel,
        out_shape=(
            pltpu.VMEM((2, 64, 512), F32),
            pltpu.VMEM((4096, 128), F32),
        ),
        in_specs=[any_space] * 3,
        out_specs=[pl.BlockSpec(memory_space=pltpu.VMEM)] * 2,
        scratch_shapes=[
            pltpu.VMEM((4096, 128), F32),
            pltpu.VMEM((512, 512), BF16),
            pltpu.VMEM((4, 512, 128), F32),
            pltpu.VMEM((NY, 16, 2, 16, 128), BF16),
            pltpu.VMEM((512, 512), F32),
            pltpu.VMEM((2, 512, 512), BF16),
            pltpu.VMEM((16, 2, NY, NZ, 16, 128), BF16),
            pltpu.VMEM((NY, NZ, 16, 128), BF16),
            pltpu.VMEM((2, NY, 64, 512), BF16),
            pltpu.VMEM((256, 1024), BF16),
            pltpu.VMEM((2, 64, 512), BF16),
            pltpu.VMEM((NY, 64, 128), F32),
            pltpu.VMEM((NY, 64, 128), F32),
            pltpu.VMEM((NY, 16, 64, 128), BF16),
            pltpu.VMEM((NY, 16, 64, 128), BF16),
            dma((3,)),
            dma,
            dma((CHUNKS, NY - 1)),
            dma((CHUNKS, NY - 1)),
            dma((2, 2)),
            dma((2, 2)),
            dma((2, CHUNKS * 2, 4)),
            dma((2, CHUNKS * 2, 4)),
            dma((2, 2, NROW)),
            dma((2, 2)),
            dma((2, NY - 1)),
            dma((2, NY - 1)),
            dma((NY - 1,)),
            dma((NY - 1,)),
            dma((NY - 1,)),
            dma((NY - 1,)),
            dma((NZ - 1,)),
            dma((NZ - 1,)),
            dma((CHUNKS, NY - 1)),
            dma((CHUNKS, NY - 1)),
        ],
        compiler_params=pltpu.CompilerParams(
            collective_id=0, has_side_effects=True, vmem_limit_bytes=48 * 1024 * 1024
        ),
        name="back_substitution",
    )(
        in_hbm(rhs.reshape(4096, 128)),
        in_hbm(factor_rows.reshape(512, 512)),
        in_hbm(diag_inverse),
    )
    return solved, updated.reshape(rhs.shape)


def solution(mesh):
    return jax.shard_map(
        on_device,
        mesh=mesh,
        in_specs=(P("col", None, "row", None), P(None, "col", None, "row", None), P()),
        out_specs=(P(None, "col", None), P("col", None, "row", None)),
        check_vma=False,
    )
```

```python
import functools

import jax
import jax.numpy as jnp
from jax import lax
from jax.experimental import pallas as pl
from jax.experimental.pallas import tpu as pltpu
from jax.sharding import PartitionSpec as P

NY, NZ, NROW = 4, 8, 8
CHUNKS = 4
UNITS = "ABCDEFGH"
ROW_TARGETS = (6, 2, 3, 0, 1, 4, 5, 7)
FAR = (2, 3, 4, 5, 6)
FARTHEST_FIRST = (2, 1, 3)
BF16, F32 = jnp.bfloat16, jnp.float32
BOUNDS = (0, 5, 9, 13, 16)
ORDER = (
    "e1", "A1", "B1", "e0", "E1", "D1", "A2", "G1", "H1", "B2", "C1",
    "n0", "A3", "D2", "edge", "C2", "A4", "E2", "solve", "B3", "F1", "C3",
    "D3", "share", "B4", "G2", "F2", "D4", "H2", "C4", "E3", "c0", "F3",
    "H3", "G3", "c1", "E4", "F4", "H4", "G4", "c2", "c3", "f0", "f1",
    "f2", "f3",
)


def kernel(
    x_hbm, f_hbm, d_hbm, sol_ref, upd_ref,
    x_v, f_v, f_wide, f_cut, d_v, d_cut, buf, edge_f, nar, lhs, low, edge_out, edge_in, back_out, back_in,
    in_sem, own_sem, ysend, yrecv, osend, orecv, zsend, zrecv, rsend, rrecv, nsend, nrecv,
    esend, erecv, pysend, pyrecv, pzsend, pzrecv, bsend, brecv,
):
    row = lax.axis_index("row")
    col = lax.axis_index("col")
    y = col // NZ
    z = col % NZ
    up, down = (z + 1) % NZ, (z + NZ - 1) % NZ
    first_root, second_root = NROW - 1, NROW - 2

    def at(row_, y_, z_):
        return (row_, y_ * NZ + z_)

    def remote(src, dst, send, recv, device):
        return pltpu.make_async_remote_copy(
            src_ref=src, dst_ref=dst, send_sem=send, recv_sem=recv,
            device_id=device, device_id_type=pl.DeviceIdType.MESH,
        )

    f_in = pltpu.make_async_copy(f_hbm, f_v, in_sem.at[0])
    x_in = pltpu.make_async_copy(x_hbm, x_v, in_sem.at[1])
    d_in = pltpu.make_async_copy(d_hbm.at[jnp.where(row == first_root, 0, 1)], d_v, in_sem.at[2])
    f_in.start()
    d_in.start()
    x_in.start()

    def signal(device):
        pl.semaphore_signal(barrier, inc=1, device_id=device, device_id_type=pl.DeviceIdType.MESH)

    barrier = pltpu.get_barrier_semaphore()
    signal(at(row, y, up))
    signal(at(row, y, down))
    for d in range(1, NY):
        signal(at(row, (y + d) % NY, z))
    for root in (first_root, second_root):
        for t in range(NROW):
            if t != root:
                if t < second_root:
                    @pl.when(row == root)
                    def _(t=t):
                        signal(at(t, y, z))

                    @pl.when(row == t)
                    def _(root=root):
                        signal(at(root, y, z))
                else:
                    @pl.when(row == root)
                    def _(t=t):
                        signal(at(t, y, z))

    @pl.when(row == second_root)
    def _():
        for d in FAR:
            signal(at(row, y, (z + d) % NZ))

    f_in.wait()
    for l in range(4):
        f_wide[l] = f_v[:, l * 128:(l + 1) * 128].astype(F32)
    for q in range(NY):
        for j in range(16):
            f_cut[q, j] = f_wide[q, pl.ds(j, 32, stride=16), :].astype(BF16).reshape(2, 16, 128)
    own = pltpu.make_async_copy(f_cut.at[y], buf.at[:, :, 0, z], own_sem)
    own.start()

    def span(c):
        return pl.ds(BOUNDS[c], BOUNDS[c + 1] - BOUNDS[c])

    def y_copy(c, d):
        to = (y + d) % NY
        return remote(
            f_cut.at[to, span(c)], buf.at[span(c), :, NY - d, z],
            ysend.at[c, d - 1], yrecv.at[c, d - 1], at(row, to, z),
        )

    def own_copy(part, way):
        blocks = span(0) if part == 0 else pl.ds(BOUNDS[1], 16 - BOUNDS[1])
        return remote(
            f_cut.at[y, blocks], buf.at[blocks, :, 0, z], osend.at[part, way], orecv.at[part, way],
            at(row, y, up if way == 0 else down),
        )

    def piece_y_copy(d):
        to = (y + d) % NY
        return remote(
            f_cut.at[to, 15, 0], edge_f.at[NY - d, z], pysend.at[d - 1], pyrecv.at[d - 1], at(row, to, z)
        )

    def piece_z_copy(d):
        return remote(
            edge_f.at[:, z], edge_f.at[:, z], pzsend.at[d - 1], pzrecv.at[d - 1], at(row, y, (z + d) % NZ)
        )

    def block_of_rhs(j):
        return jnp.concatenate(
            [x_v[pl.ds(4 * j + l, 64, stride=64), :] for l in range(4)], axis=1
        )

    def halves(value):
        high = value.astype(BF16)
        return high, (value - high.astype(F32)).astype(BF16)

    def times_inverse(value):
        high, rest = halves(value)
        dot = functools.partial(jnp.dot, preferred_element_type=F32)
        return dot(high, d_cut[0]) + (dot(high, d_cut[1]) + dot(rest, d_cut[0]))

    def spread_row(s, root):
        for part in range(2):
            for t in ROW_TARGETS:
                if t != root:
                    row_copy(s, part, t).start()

    def row_copy(s, part, t):
        ref = nar.at[s, y] if part == 0 else low.at[s]
        return remote(ref, ref, rsend.at[s, part, t], rrecv.at[s, part], at(t, y, z))

    def narrow_copy(s, d):
        ref = nar.at[s, y]
        return remote(ref, ref, nsend.at[s, d - 1], nrecv.at[s, d - 1], at(row, (y + d) % NY, z))

    def share_narrow(s, root):
        @pl.when(row != root)
        def _():
            row_copy(s, 0, 0).wait_recv()

        for d in FARTHEST_FIRST:
            narrow_copy(s, d).start()

    def take_narrow(s):
        for d in range(1, NY):
            narrow_copy(s, d).wait_recv()
        for d in range(NY):
            columns = pl.ds(pl.multiple_of((y + d) % NY * 128, 128), 128)
            for q in range(NY):
                lhs[q * 64:(q + 1) * 64, s * 512 + d * 128:s * 512 + (d + 1) * 128] = nar[s, q, :, columns]

    def store_solved(s, root):
        @pl.when(row != root)
        def _():
            row_copy(s, 1, 0).wait_recv()

        sol_ref[s] = nar[s, y].astype(F32) + low[s].astype(F32)

    @pl.when(row == first_root)
    def _():
        pl.semaphore_wait(barrier, 2 + NY - 1 + NROW - 1)

    @pl.when(row == second_root)
    def _():
        pl.semaphore_wait(barrier, 2 + NY - 1 + NROW - 1 + len(FAR))
        for d in range(1, NY):
            piece_y_copy(d).start()
        edge_f[0, z] = f_cut[y, 15, 0]

    @pl.when(row < second_root)
    def _():
        pl.semaphore_wait(barrier, 2 + NY - 1 + 2)

    for c in range(CHUNKS):
        for d in FARTHEST_FIRST:
            y_copy(c, d).start()
        if c < 2:
            for way in range(2):
                own_copy(c, way).start()

    d_in.wait()
    x_in.wait()

    @pl.when(row >= second_root)
    def _():
        for i in range(4):
            rows = slice(i * 128, (i + 1) * 128)
            d_cut[0, rows], d_cut[1, rows] = halves(d_v[rows])

    @pl.when(row == first_root)
    def _():
        nar[0, y], low[0] = halves(times_inverse(block_of_rhs(15)))
        spread_row(0, first_root)

    def hop_copy(unit, hop, way):
        c, s = unit
        n = c * 2 + s
        block = (z - (hop - 1) + NZ) % NZ if way == 0 else (z + hop - 1) % NZ
        if hop == 1:
            ref = buf.at[span(c), s, pl.ds(1, NY - 1), block]
        elif hop < 4:
            ref = buf.at[span(c), s, :, block]
        else:
            ref = buf.at[span(c), s, pl.ds(2 * way, 2), block]
        return remote(
            ref, ref, zsend.at[way, n, hop - 1], zrecv.at[way, n, hop - 1],
            at(row, y, up if way == 0 else down),
        )

    def edge_copy(d):
        to = (y + d) % NY
        return remote(edge_out.at[to], edge_in.at[y], esend.at[d - 1], erecv.at[d - 1], at(row, to, z))

    def back_copy(c, d):
        to = (y + d) % NY
        return remote(
            back_out.at[to, span(c)], back_in.at[y, span(c)], bsend.at[c, d - 1], brecv.at[c, d - 1], at(row, to, z)
        )

    def wait_last(unit):
        for way in range(2):
            hop_copy(unit, 4, way).wait_recv()

    def subtract(j, q, change):
        rows = pl.ds(4 * j + q, 64, stride=64)
        upd_ref[rows, :] = x_v[rows, :] - change.astype(F32)

    own_seen, y_seen = set(), set()
    multiplied = stored = False
    own.wait()
    for step in ORDER:
        if step[0] in UNITS and len(step) == 2:
            n = UNITS.index(step[0])
            unit, hop = (n // 2, n % 2), int(step[1])
            c = unit[0]
            if hop == 1 and c not in y_seen:
                y_seen.add(c)
                for d in range(1, NY):
                    y_copy(c, d).wait_recv()
            if hop == 2 and min(c, 1) not in own_seen:
                own_seen.add(min(c, 1))
                for way in range(2):
                    own_copy(min(c, 1), way).wait_recv()
            for way in range(2):
                if hop > 1:
                    hop_copy(unit, hop - 1, way).wait_recv()
                hop_copy(unit, hop, way).start()
        elif step == "e0":

            @pl.when(row >= second_root)
            def _():
                share_narrow(0, first_root)

        elif step == "e1":

            @pl.when(row == second_root)
            def _():
                for d in range(1, NY):
                    piece_y_copy(d).wait_recv()
                for d in range(1, NZ):
                    piece_z_copy(d).start()

        elif step == "n0":

            @pl.when(row < second_root)
            def _():
                share_narrow(0, first_root)

        elif step == "edge":

            @pl.when(row == second_root)
            def _():
                take_narrow(0)
                for d in range(1, NZ):
                    piece_z_copy(d).wait_recv()
                product = jnp.dot(
                    lhs[:, :512], edge_f[...].reshape(512, 128), preferred_element_type=F32
                )
                edge_out[...] = product.reshape(NY, 64, 128)
                for d in range(1, NY):
                    edge_copy(d).start()
                edge_in[y] = edge_out[y]

        elif step == "solve":

            @pl.when(row == second_root)
            def _():
                for d in range(1, NY):
                    edge_copy(d).wait_recv()
                change = jnp.concatenate([edge_in[q] for q in range(NY)], axis=1)
                nar[1, y], low[1] = halves(times_inverse(block_of_rhs(15) - change))
                spread_row(1, second_root)

        elif step == "share":
            share_narrow(1, second_root)
        elif step[0] == "c":
            c = int(step[1])
            if not multiplied:
                multiplied = True

                @pl.when(row != second_root)
                def _():
                    take_narrow(0)

                take_narrow(1)
            for s in range(2):
                wait_last((c, s))
            for j in range(BOUNDS[c], BOUNDS[c + 1], 2):
                width = min(2, BOUNDS[c + 1] - j)
                factor = jnp.concatenate([buf[j + i].reshape(1024, 128) for i in range(width)], axis=1)
                change = jnp.dot(lhs[...], factor, preferred_element_type=F32).astype(BF16)
                for i in range(width):
                    back_out[:, j + i] = change[:, i * 128:(i + 1) * 128].reshape(NY, 64, 128)
            for d in FARTHEST_FIRST:
                back_copy(c, d).start()
        else:
            c = int(step[1])
            if not stored:
                stored = True
                for s in range(2):
                    store_solved(s, NROW - 1 - s)
            for d in range(1, NY):
                back_copy(c, d).wait_recv()
            back_in[y, span(c)] = back_out[y, span(c)]
            for q in range(NY):
                for j in range(BOUNDS[c], BOUNDS[c + 1]):
                    if j < 15:
                        subtract(j, q, back_in[q, j])
                    else:
                        @pl.when(row < second_root)
                        def _(q=q):
                            subtract(15, q, back_in[q, 15])

                        @pl.when(row == second_root)
                        def _(q=q):
                            subtract(15, q, edge_in[q])

                        @pl.when(row == first_root)
                        def _(q=q):
                            subtract(15, q, jnp.zeros((64, 128), F32))

    for c in range(CHUNKS):
        for d in range(1, NY):
            y_copy(c, d).wait_send()
            back_copy(c, d).wait_send()
        for s in range(2):
            for hop in range(1, 5):
                for way in range(2):
                    hop_copy((c, s), hop, way).wait_send()
    for part in range(2):
        for way in range(2):
            own_copy(part, way).wait_send()
    for s in range(2):
        for d in range(1, NY):
            narrow_copy(s, d).wait_send()
    for s in range(2):
        root = NROW - 1 - s

        @pl.when(row == root)
        def _():
            for part in range(2):
                for t in range(NROW):
                    if t != root:
                        row_copy(s, part, t).wait_send()

    @pl.when(row == second_root)
    def _():
        for d in range(1, NY):
            piece_y_copy(d).wait_send()
            edge_copy(d).wait_send()
        for d in range(1, NZ):
            piece_z_copy(d).wait_send()


def on_device(rhs, factor_rows, diag_inverse):
    dma = pltpu.SemaphoreType.DMA
    any_space = pl.BlockSpec(memory_space=pl.ANY)
    in_hbm = functools.partial(pltpu.with_memory_space_constraint, memory_space=pltpu.HBM)
    solved, updated = pl.pallas_call(
        kernel,
        out_shape=(
            pltpu.VMEM((2, 64, 512), F32),
            pltpu.VMEM((4096, 128), F32),
        ),
        in_specs=[any_space] * 3,
        out_specs=[pl.BlockSpec(memory_space=pltpu.VMEM)] * 2,
        scratch_shapes=[
            pltpu.VMEM((4096, 128), F32),
            pltpu.VMEM((512, 512), BF16),
            pltpu.VMEM((4, 512, 128), F32),
            pltpu.VMEM((NY, 16, 2, 16, 128), BF16),
            pltpu.VMEM((512, 512), F32),
            pltpu.VMEM((2, 512, 512), BF16),
            pltpu.VMEM((16, 2, NY, NZ, 16, 128), BF16),
            pltpu.VMEM((NY, NZ, 16, 128), BF16),
            pltpu.VMEM((2, NY, 64, 512), BF16),
            pltpu.VMEM((256, 1024), BF16),
            pltpu.VMEM((2, 64, 512), BF16),
            pltpu.VMEM((NY, 64, 128), F32),
            pltpu.VMEM((NY, 64, 128), F32),
            pltpu.VMEM((NY, 16, 64, 128), BF16),
            pltpu.VMEM((NY, 16, 64, 128), BF16),
            dma((3,)),
            dma,
            dma((CHUNKS, NY - 1)),
            dma((CHUNKS, NY - 1)),
            dma((2, 2)),
            dma((2, 2)),
            dma((2, CHUNKS * 2, 4)),
            dma((2, CHUNKS * 2, 4)),
            dma((2, 2, NROW)),
            dma((2, 2)),
            dma((2, NY - 1)),
            dma((2, NY - 1)),
            dma((NY - 1,)),
            dma((NY - 1,)),
            dma((NY - 1,)),
            dma((NY - 1,)),
            dma((NZ - 1,)),
            dma((NZ - 1,)),
            dma((CHUNKS, NY - 1)),
            dma((CHUNKS, NY - 1)),
        ],
        compiler_params=pltpu.CompilerParams(
            collective_id=0, has_side_effects=True, vmem_limit_bytes=48 * 1024 * 1024
        ),
        name="back_substitution",
    )(
        in_hbm(rhs.reshape(4096, 128)),
        in_hbm(factor_rows.reshape(512, 512)),
        in_hbm(diag_inverse),
    )
    return solved, updated.reshape(rhs.shape)


def solution(mesh):
    return jax.shard_map(
        on_device,
        mesh=mesh,
        in_specs=(P("col", None, "row", None), P(None, "col", None, "row", None), P()),
        out_specs=(P(None, "col", None), P("col", None, "row", None)),
        check_vma=False,
    )
```
